128 devices in a mesh: row: 8 (over y, core), col: 16 (over z, x).
Axes of the slice: x: 4, y: 4, z: 4, core: 2. Of those that a mesh axis runs over, the one named last changes fastest.
Arguments:
- integrals: bfloat16 [1024, 512, 256], P('row', 'col'), may hold values from -0.625 to 0.625
- virt_green: bfloat16 [512, 512], P('col'), may hold values from -0.375 to 0.375
- occ_green: bfloat16 [512, 512], P('col'), may hold values from -0.375 to 0.375
- block_list: int32 [16, 8], replicated, may hold values from 0 to 15, as said below
- block_owner: int32 [16], replicated, may hold values from 0 to 15, each once
- block_sizes: int32 [16], replicated, may hold values from 16 to 32
Outputs:
- response: float32 [1024, 1024], P('row', 'col')
The draws below stay inside these ranges and needn't reach their ends.
Inputs may be any that keep to these rules, and one draw needn't show every extreme that they name: `block_list`: each row names 8 different atoms.
All inputs are finite; a program needn't handle non-finite values.
Results may differ from the reference program's by a relative error of at most 0.0041.
Values may be sent and summed in bfloat16 or wider, within the bound.
A program may use at most 128 MiB of HBM per device.

```python
import jax
import jax.numpy as jnp
from jax import lax

BS = 32
K = 8
NATOM = 16
NORB = 512
NAUX = 1024


def draw_block_list(key, part):
    key = jax.random.fold_in(key, 7)
    keys = jax.random.split(key, NATOM)
    lists = jax.vmap(lambda single: jax.random.permutation(single, NATOM)[:K])(keys)
    return lists.astype(jnp.int32)


def touch_ends(result, rng, smallest, high):
    spot = [jax.random.randint(jax.random.fold_in(rng, axis), (), 0, length) for axis, length in enumerate(result.shape)]
    widest = result.shape.index(max(result.shape))
    next_to = spot[:widest] + [(spot[widest] + 1) % result.shape[widest]] + spot[widest + 1:]
    return result.at[tuple(spot)].set(smallest).at[tuple(next_to)].set(high)


def levels(rng, extent, shards, low, high):
    def one(axis_at, shards_of):
        steps = jax.random.uniform(jax.random.fold_in(jax.random.fold_in(rng, 6), axis_at), (shards_of,), jnp.float32, low / len(shards), high / len(shards))
        return jnp.repeat(jnp.exp(steps), extent[axis_at] // shards_of).reshape((-1,) + (1,) * (len(extent) - axis_at - 1))

    level = one(*shards[0])
    for cut in shards[1:]:
        level = level * one(*cut)
    return level


def normal_values(own_key, shape, deviation, bound, pieces=(), kind=jnp.bfloat16):
    values = jax.random.normal(own_key, shape, jnp.float32) * deviation
    if len(pieces) > 0:
        values = levels(own_key, shape, pieces, -0.22, 0.18) * values
    return jnp.clip(values, min=-bound, max=bound).astype(kind)


def setup_inputs(seed: int = 0) -> dict:
    splits = jax.random.split(jax.random.key(seed), 7)
    return {
        "integrals": normal_values(splits[0], (NAUX, NORB, K * BS), (NORB ** -0.5), 0.625, ((0, 8), (1, 16))),
        "virt_green": normal_values(splits[1], (NORB, NORB), (K * BS) ** -0.5, 0.375, ((0, 16),)),
        "occ_green": normal_values(splits[2], (NORB, NORB), (K * BS) ** -0.5, 0.375, ((0, 16),)),
        "block_list": draw_block_list(jax.random.fold_in(splits[6], 71), 0),
        "block_owner": jax.random.permutation(splits[4], NATOM).astype(jnp.int32),
        "block_sizes": touch_ends(jax.random.randint(splits[5], (NATOM,), BS // 2, BS + 1), jax.random.fold_in(splits[5], 1), BS // 2, BS).astype(jnp.int32),
    }


def slot_atoms(block_owner):
    ids = jnp.arange(NATOM, dtype=jnp.int32)
    match = block_owner[:, None] == ids[None, :]
    return jnp.sum(jnp.where(match, ids[:, None], 0), axis=0).astype(jnp.int32)


def valid_mask(atoms, block_sizes):
    sizes = block_sizes[atoms]
    inside = jnp.arange(BS, dtype=jnp.int32)[None, :] < sizes[:, None]
    return inside.reshape(NORB)


def reference(integrals, virt_green, occ_green, block_list, block_owner, block_sizes):
    atoms = slot_atoms(block_owner)
    valid = valid_mask(atoms, block_sizes)
    both = valid[:, None] & valid[None, :]
    virt_eff = jnp.where(both, virt_green, jnp.zeros_like(virt_green))
    occ_eff = jnp.where(both, occ_green, jnp.zeros_like(occ_green))
    owners = block_owner[block_list[atoms]]
    row_index = (owners[:, :, None] * BS + jnp.arange(BS, dtype=jnp.int32)[None, None, :]).reshape(NATOM, K * BS)
    blocks = integrals.reshape(NAUX, NATOM, BS, K * BS).transpose(1, 0, 2, 3)

    def factors(item):
        block, index = item
        flat = block.reshape(NAUX * BS, K * BS)
        left = jnp.dot(flat, jnp.take(virt_eff, index, axis=0), preferred_element_type=jnp.float32)
        right = jnp.dot(flat, jnp.take(occ_eff, index, axis=0), preferred_element_type=jnp.float32)
        return left.astype(jnp.bfloat16), right.astype(jnp.bfloat16)

    left_all, right_all = lax.map(factors, (blocks, row_index))
    left = left_all.reshape(NATOM, NAUX, BS, NORB).transpose(1, 0, 2, 3).reshape(NAUX, NORB * NORB)
    right = right_all.reshape(NATOM, NAUX, BS, NORB).transpose(1, 3, 0, 2).reshape(NAUX, NORB * NORB)
    return jnp.dot(left, right.T, preferred_element_type=jnp.float32)
```

```python
import jax
import jax.numpy as jnp
from jax import lax
from jax.experimental import pallas as pl
from jax.experimental.pallas import tpu as pltpu
from jax.sharding import PartitionSpec as P

BF = jnp.bfloat16
F32 = jnp.float32
ANY = pl.BlockSpec(memory_space=pl.ANY)
VMEM = pl.BlockSpec(memory_space=pltpu.VMEM)
SMEM = pl.BlockSpec(memory_space=pltpu.SMEM)
ROWS, COLS, YS = 8, 16, 4


def place():
    r = lax.axis_index("row")
    c = lax.axis_index("col")
    return r, c, r // 2, r % 2


def loop(lo, hi, body):
    def step(i, carry):
        body(i)
        return carry

    lax.fori_loop(lo, hi, step, 0)


def remote(src, dst, ssem, rsem, row, col):
    return pltpu.make_async_remote_copy(
        src_ref=src, dst_ref=dst, send_sem=ssem, recv_sem=rsem,
        device_id=(row, col), device_id_type=pl.DeviceIdType.MESH,
    )


def spread_kernel(ints, virt, occ, vall, oall, mine, quart,
                  vs, vr, os_, or_, ms, mr, qs, qr, fs, fr, loc):
    r, c, y, core = place()

    def green(src, dst, s, q, k):
        to = (c + k) % COLS
        return remote(src, dst.at[pl.ds(c * 32, 32)], s.at[k], q.at[k], r, to)

    def block(k):
        to = (c + k) % COLS
        return remote(ints.at[pl.ds(to * 8, 8)], mine.at[c], ms.at[k], mr.at[k], r, to)

    def piece(yy):
        return ints.at[:, pl.ds((yy // 2) * 16, 16), pl.ds((yy % 2) * 128, 128)]

    def quarter(k):
        to = (y + k) % YS
        return remote(piece(to), quart.at[r], qs.at[k], qr.at[k], to * 2 + core, c)

    def forward(k):
        frm = ((y + YS - k) % YS) * 2 + core
        return remote(quart.at[frm], quart.at[frm], fs.at[k], fr.at[k], y * 2 + (1 - core), c)

    def own(k):
        return remote(piece(y), quart.at[r], fs.at[0], fr.at[0], y * 2 + (1 - core), c)

    loop(1, COLS, lambda k: (green(virt, vall, vs, vr, k).start(), green(occ, oall, os_, or_, k).start()))
    loop(1, YS, lambda k: quarter(k).start())
    loop(1, COLS, lambda k: block(k).start())
    copies = [
        pltpu.make_async_copy(virt, vall.at[pl.ds(c * 32, 32)], loc.at[0]),
        pltpu.make_async_copy(occ, oall.at[pl.ds(c * 32, 32)], loc.at[1]),
        pltpu.make_async_copy(ints.at[pl.ds(c * 8, 8)], mine.at[c], loc.at[2]),
        pltpu.make_async_copy(piece(y), quart.at[r], loc.at[3]),
    ]
    for copy in copies:
        copy.start()
    own(0).start()

    def pass_on(k):
        quarter(k).wait_recv()
        forward(k).start()

    loop(1, YS, pass_on)
    for copy in copies:
        copy.wait()
    loop(1, COLS, lambda k: (green(virt, vall, vs, vr, k).wait(), green(occ, oall, os_, or_, k).wait()))
    loop(1, COLS, lambda k: block(k).wait())
    loop(1, YS, lambda k: quarter(k).wait_send())
    loop(1, YS, lambda k: forward(k).wait())
    own(0).wait()


def spread(ints, virt, occ):
    dma = pltpu.SemaphoreType.DMA
    return pl.pallas_call(
        spread_kernel,
        out_shape=(
            jax.ShapeDtypeStruct((512, 512), BF),
            jax.ShapeDtypeStruct((512, 512), BF),
            jax.ShapeDtypeStruct((16, 8, 32, 256), BF),
            jax.ShapeDtypeStruct((8, 128, 16, 128), BF),
        ),
        in_specs=[ANY] * 3,
        out_specs=(ANY,) * 4,
        scratch_shapes=[dma((16,))] * 6 + [dma((4,))] * 4 + [dma((4,))],
        compiler_params=pltpu.CompilerParams(has_side_effects=True),
    )(ints, virt, occ)


def factor_kernel(lists, owner, sizes, mine, virt, occ, out, atom, veff, oeff, left, left_t):
    for a in range(16):
        atom[owner[a]] = a
    lane = lax.broadcasted_iota(jnp.int32, (32, 512), 1)
    row = lax.broadcasted_iota(jnp.int32, (32, 512), 0)
    limit = jnp.zeros((32, 512), jnp.int32)
    for s in range(16):
        limit = jnp.where(lane // 32 == s, sizes[atom[s]], limit)
    inside = lane % 32 < limit
    for s in range(16):
        both = jnp.logical_and(inside, row < sizes[atom[s]])
        rows = pl.ds(s * 32, 32)
        veff[rows, :] = jnp.where(both, virt[rows, :], jnp.zeros((), BF))
        oeff[rows, :] = jnp.where(both, occ[rows, :], jnp.zeros((), BF))

    def listed(ref, s):
        a = atom[s]
        parts = [ref[pl.ds(pl.multiple_of(owner[lists[a, k]] * 32, 32), 32), :] for k in range(8)]
        return jnp.concatenate(parts, axis=0)

    def make_left(s):
        lhs = mine[s].reshape(256, 256)
        res = jnp.dot(lhs, listed(veff, s), preferred_element_type=F32).astype(BF)
        left[:, pl.ds(pl.multiple_of(s * 32, 32), 32), :] = res.reshape(8, 32, 512)

    loop(0, 16, make_left)

    def turn(p):
        left_t[p] = left[p].T

    loop(0, 8, turn)

    def make_out(t):
        lhs = left_t[:, pl.ds(pl.multiple_of(t * 32, 32), 32), :].reshape(256, 512)
        res = lax.dot_general(lhs, listed(oeff, t), (((1,), (1,)), ((), ())), preferred_element_type=F32)
        out[t] = res.astype(BF).reshape(8, 32, 256)

    loop(0, 16, make_out)


def factors(lists, owner, sizes, mine, virt, occ):
    return pl.pallas_call(
        factor_kernel,
        out_shape=jax.ShapeDtypeStruct((16, 8, 32, 256), BF),
        in_specs=[SMEM] * 3 + [VMEM] * 3,
        out_specs=VMEM,
        scratch_shapes=[
            pltpu.SMEM((16,), jnp.int32),
            pltpu.VMEM((512, 512), BF),
            pltpu.VMEM((512, 512), BF),
            pltpu.VMEM((8, 512, 512), BF),
            pltpu.VMEM((8, 512, 512), BF),
        ],
        compiler_params=pltpu.CompilerParams(vmem_limit_bytes=40 << 20),
    )(lists, owner, sizes, mine, virt, occ)


def finish_kernel(w, quart, out, wgot, qv, i2, w2, part, got, ws, wr, ps, pr, loc):
    r, c, y, core = place()
    me = y * COLS + c

    def send_w(k):
        to = (me + k) % 64
        yy, cc = to // COLS, to % COLS
        src = w.at[cc, :, pl.ds((yy // 2) * 16, 16), pl.ds((yy % 2) * 128, 128)]
        return remote(src, wgot.at[me], ws.at[k], wr.at[k], yy * 2 + core, cc)

    def send_part(k):
        to = (me + k) % 64
        yy, cc = to // COLS, to % COLS
        src = part.at[cc, :, pl.ds(pl.multiple_of(yy * 128, 128), 128)]
        return remote(src, got.at[me], ps.at[k], pr.at[k], yy * 2 + core, cc)

    loop(1, 64, lambda k: send_w(k).start())
    own = pltpu.make_async_copy(
        w.at[c, :, pl.ds((y // 2) * 16, 16), pl.ds((y % 2) * 128, 128)], wgot.at[me], loc.at[0])
    own.start()
    load = pltpu.make_async_copy(quart, qv, loc.at[1])
    load.start()
    a = lax.broadcasted_iota(jnp.int32, (256, 256), 0)
    b = lax.broadcasted_iota(jnp.int32, (256, 256), 1)
    perm = jnp.where((a // 16 == b % 16) & (a % 16 == b // 16), 1.0, 0.0).astype(BF)
    load.wait()

    def spread_rows(x, dst, at):
        x = jnp.dot(perm, x, preferred_element_type=F32).astype(BF)
        for j in range(16):
            dst[pl.ds(at, 16), j * 128:(j + 1) * 128] = x[j * 16:(j + 1) * 16, :]

    def lay_i(i):
        x = qv[i // 8, pl.ds(pl.multiple_of(i % 8 * 16, 16), 16)].reshape(256, 128)
        spread_rows(x, i2, pl.multiple_of(i * 16, 16))

    loop(0, 64, lay_i)
    loop(1, 64, lambda k: send_w(k).wait())
    own.wait()

    def lay_w(i):
        x = wgot[pl.ds(i * 2, 2)].reshape(256, 128)
        spread_rows(x, w2, pl.multiple_of(i * 16, 16))

    loop(0, 32, lay_w)

    def multiply(i):
        x = i2[pl.ds(pl.multiple_of(i * 256, 256), 256), :]
        res = lax.dot_general(x, w2[...], (((1,), (1,)), ((), ())), preferred_element_type=F32)
        part[pl.ds(i * 4, 4)] = res.astype(BF).reshape(4, 64, 512)

    loop(0, 4, multiply)
    loop(1, 64, lambda k: send_part(k).start())
    keep = pltpu.make_async_copy(
        part.at[c, :, pl.ds(pl.multiple_of(y * 128, 128), 128)], got.at[me], loc.at[2])
    keep.start()
    loop(1, 64, lambda k: send_part(k).wait())
    keep.wait()
    total = lax.fori_loop(0, 64, lambda i, acc: acc + got[i].astype(F32), jnp.zeros((64, 128), F32))
    out[...] = total.T


def finish(w, quart):
    dma = pltpu.SemaphoreType.DMA
    return pl.pallas_call(
        finish_kernel,
        out_shape=jax.ShapeDtypeStruct((128, 64), F32),
        in_specs=[ANY] * 2,
        out_specs=VMEM,
        scratch_shapes=[
            pltpu.VMEM((64, 8, 16, 128), BF),
            pltpu.VMEM((8, 128, 16, 128), BF),
            pltpu.VMEM((1024, 2048), BF),
            pltpu.VMEM((512, 2048), BF),
            pltpu.VMEM((16, 64, 512), BF),
            pltpu.VMEM((64, 64, 128), BF),
        ] + [dma((64,))] * 4 + [dma((3,))],
        compiler_params=pltpu.CompilerParams(has_side_effects=True, vmem_limit_bytes=40 << 20),
    )(w, quart)


def shards(integrals, virt_green, occ_green, block_list, block_owner, block_sizes):
    vall, oall, mine, quart = spread(integrals, virt_green, occ_green)
    w = factors(block_list, block_owner, block_sizes, mine, vall, oall)
    return finish(w, quart)


def solution(mesh):
    in_specs = (P("row", "col", None), P("col", None), P("col", None), P(), P(), P())
    return jax.shard_map(shards, mesh=mesh, in_specs=in_specs, out_specs=P("row", "col"), check_vma=False)
```

```python
import jax
import jax.numpy as jnp
from jax import lax
from jax.experimental import pallas as pl
from jax.experimental.pallas import tpu as pltpu
from jax.sharding import PartitionSpec as P

BF = jnp.bfloat16
F32 = jnp.float32
ANY = pl.BlockSpec(memory_space=pl.ANY)
VMEM = pl.BlockSpec(memory_space=pltpu.VMEM)
SMEM = pl.BlockSpec(memory_space=pltpu.SMEM)
MESH = pl.DeviceIdType.MESH
NT = (((1,), (1,)), ((), ()))
ORDER = (10, 15, 4, 9, 14, 3, 8, 13, 2, 7, 12, 1, 6, 11, 5)


def loop(lo, hi, body, unroll=1):
    def step(i, carry):
        body(i)
        return carry

    lax.fori_loop(lo, hi, step, 0, unroll=unroll)


def remote(src, dst, ssem, rsem, row, col):
    return pltpu.make_async_remote_copy(
        src_ref=src, dst_ref=dst, send_sem=ssem, recv_sem=rsem, device_id=(row, col), device_id_type=MESH,
    )


def arrived(ref, sem):
    pltpu.make_async_copy(ref, ref, sem).wait()


def kernel(lists, owner, sizes, ints, virt, occ, out,
           starts, slot_size, gsrc, green, mine, quart, veff, oeff, left, left_t, wout, wgot, i2, w2, part, got,
           g1s, g1r, g2s, g2r, g3s, g3r, ms, mr, qs, qr, fs, fr, ws, wr, ps, pr, loc):
    r = lax.axis_index("row")
    c = lax.axis_index("col")
    y, core = r // 2, r % 2
    z, x = c // 4, c % 4
    me = y * 16 + c
    twin = y * 2 + (1 - core)

    def col_to(k):
        return (z + k // 4) % 4 * 4 + (x + k % 4) % 4

    def col_from(k):
        return (z + 4 - k // 4) % 4 * 4 + (x + 4 - k % 4) % 4

    def row_to(k):
        return (y + k) % 4 * 2 + core

    def piece(yy):
        return ints.at[:, pl.ds((yy // 2) * 16, 16), pl.ds((yy % 2) * 128, 128)]

    def green1(k):
        src = gsrc.at[core, :, pl.ds(pl.multiple_of(y * 128, 128), 128)]
        return remote(src, green.at[core, y, pl.ds(c * 32, 32)], g1s.at[k], g1r.at[k], r, col_to(k))

    def green2(k):
        return remote(green.at[core, y], green.at[core, y], g2s.at[k], g2r.at[k], row_to(k), c)

    def green3(k):
        q = (y + 4 - k) % 4
        return remote(green.at[core, q], green.at[core, q], g3s.at[k], g3r.at[k], twin, c)

    def block(k):
        return remote(ints.at[pl.ds(col_to(k) * 8, 8)], mine.at[c], ms.at[k], mr.at[k], r, col_to(k))

    def quarter(k):
        return remote(piece((y + k) % 4), quart.at[r], qs.at[k], qr.at[k], row_to(k), c)

    def forward(k):
        frm = (y + 4 - k) % 4 * 2 + core
        return remote(quart.at[frm], quart.at[frm], fs.at[k], fr.at[k], twin, c)

    def send_own():
        return remote(piece(y), quart.at[r], fs.at[0], fr.at[0], twin, c)

    def send_w(k):
        yy, cc = (y + k // 16) % 4, col_to(k % 16)
        src = wout.at[cc, :, pl.ds((yy // 2) * 16, 16), pl.ds((yy % 2) * 128, 128)]
        return remote(src, wgot.at[me], ws.at[k], wr.at[k], yy * 2 + core, cc)

    def send_part(k):
        yy, cc = (y + k // 16) % 4, col_to(k % 16)
        src = part.at[cc, :, pl.ds(pl.multiple_of(yy * 128, 128), 128)]
        return remote(src, got.at[me], ps.at[k], pr.at[k], yy * 2 + core, cc)

    own = [
        pltpu.make_async_copy(virt, gsrc.at[0], loc.at[0]),
        pltpu.make_async_copy(occ, gsrc.at[1], loc.at[1]),
        pltpu.make_async_copy(ints.at[pl.ds(c * 8, 8)], mine.at[c], mr.at[0]),
        pltpu.make_async_copy(piece(y), quart.at[r], qr.at[0]),
    ]
    for copy in own:
        copy.start()

    barrier = pltpu.get_barrier_semaphore()

    def greet(row, col):
        pl.semaphore_signal(barrier, inc=1, device_id=(row, col), device_id_type=MESH)

    loop(1, 16, lambda k: greet(r, col_to(k)))
    loop(1, 4, lambda k: greet(row_to(k), c))
    greet(twin, c)
    pl.semaphore_wait(barrier, 19)

    own[0].wait()
    own[1].wait()
    keep = pltpu.make_async_copy(
        gsrc.at[core, :, pl.ds(pl.multiple_of(y * 128, 128), 128)], green.at[core, y, pl.ds(c * 32, 32)], g1r.at[0])
    keep.start()
    for k in ORDER:
        green1(k).start()
    for k in (2, 1, 3):
        quarter(k).start()
    for k in ORDER:
        block(k).start()
    send_own().start()

    for s in range(16):
        atom = jnp.int32(0)
        for a in range(16):
            atom = jnp.where(owner[a] == s, a, atom)
        slot_size[s] = sizes[atom]
        for k in range(8):
            starts[s * 8 + k] = owner[lists[atom, k]]

    keep.wait()
    loop(1, 16, lambda k: green1(k).wait_recv())
    loop(1, 4, lambda k: green2(k).start())
    green3(0).start()

    def pass_green(k):
        green2(k).wait_recv()
        green3(k).start()

    loop(1, 4, pass_green)
    loop(0, 4, lambda k: green3(k).wait_recv())

    lane = lax.broadcasted_iota(jnp.int32, (32, 128), 1)
    row = lax.broadcasted_iota(jnp.int32, (32, 128), 0)
    for q in range(4):
        limit = jnp.zeros((32, 128), jnp.int32)
        for s in range(4):
            limit = jnp.where(lane // 32 == s, slot_size[q * 4 + s], limit)
        inside = lane % 32 < limit
        for s in range(16):
            both = jnp.logical_and(inside, row < slot_size[s])
            rows = pl.ds(s * 32, 32)
            veff[s, :, q * 128:(q + 1) * 128] = jnp.where(both, green[0, q, rows, :], jnp.zeros((), BF))
            oeff[s, :, q * 128:(q + 1) * 128] = jnp.where(both, green[1, q, rows, :], jnp.zeros((), BF))

    def listed(ref, s):
        return jnp.concatenate([ref[starts[s * 8 + k]] for k in range(8)], axis=0)

    def make_left(dz):
        zz = (z + 4 - dz) % 4
        for dx in range(4):
            arrived(mine.at[zz * 4 + (x + 4 - dx) % 4], mr.at[dz * 4 + dx])
        for xx in range(4):
            s = zz * 4 + xx
            res = jnp.dot(mine[s].reshape(256, 256), listed(veff, s), preferred_element_type=F32)
            left[:, xx * 32:(xx + 1) * 32, :] = res.astype(BF).reshape(8, 32, 512)
        for p in range(8):
            left_t[p, :, pl.ds(pl.multiple_of(zz * 128, 128), 128)] = left[p].T

    loop(0, 4, make_left)

    def make_w(k):
        t = col_to(k)
        lhs = left_t[:, pl.ds(pl.multiple_of(t * 32, 32), 32), :].reshape(256, 512)
        res = lax.dot_general(lhs, listed(oeff, t), NT, preferred_element_type=F32)
        wout[t] = res.astype(BF).reshape(8, 32, 256)

    for k in ORDER:
        make_w(k)
        for dy in (2, 1, 3, 0):
            send_w(dy * 16 + k).start()
    make_w(0)
    for dy in (2, 1, 3):
        send_w(dy * 16).start()
    keep_w = pltpu.make_async_copy(
        wout.at[c, :, pl.ds((y // 2) * 16, 16), pl.ds((y % 2) * 128, 128)], wgot.at[me], wr.at[0])
    keep_w.start()

    def pass_quarter(k):
        quarter(k).wait_recv()
        forward(k).start()

    loop(1, 4, pass_quarter)
    own[3].wait()

    def lay_i(i):
        v = jnp.swapaxes(quart[i // 8, pl.ds(pl.multiple_of(i % 8 * 16, 16), 16)], 0, 1)
        for j in range(16):
            i2[pl.ds(pl.multiple_of(i * 16, 16), 16), j * 128:(j + 1) * 128] = v[j]

    def lay_piece(rr):
        loop(rr * 8, rr * 8 + 8, lay_i)

    loop(0, 4, lambda k: lay_piece(row_to(k)))

    def lay_other(k):
        forward(k).wait_recv()
        lay_piece((y + 4 - k) % 4 * 2 + 1 - core)

    loop(0, 4, lay_other)

    def lay_w(i):
        yy = (y + 4 - i // 8) % 4
        zz = (z + 4 - i // 2 % 4) % 4
        for h in range(2):
            xx = i % 2 * 2 + h
            k = i // 8 * 16 + i // 2 % 4 * 4 + (x + 4 - xx) % 4
            arrived(wgot.at[yy * 16 + zz * 4 + xx], wr.at[k])
        pair = yy * 8 + zz * 2 + i % 2
        v = jnp.swapaxes(wgot[pl.ds(pair * 2, 2)].reshape(16, 16, 128), 0, 1)
        for j in range(16):
            w2[pl.ds(pl.multiple_of(pair * 16, 16), 16), j * 128:(j + 1) * 128] = v[j]

    loop(0, 32, lay_w)

    def multiply(dz):
        zz = (z + dz) % 4
        v = i2[pl.ds(pl.multiple_of(zz * 256, 256), 256), :]
        res = lax.dot_general(v, w2[...], NT, preferred_element_type=F32)
        part[pl.ds(zz * 4, 4)] = res.astype(BF).reshape(4, 64, 512)

    for dz in (2, 1, 3, 0):
        multiply(dz)
        for dx in (2, 1, 3, 0):
            for dy in (2, 1, 3, 0):
                k = dy * 16 + dz * 4 + dx
                if k:
                    send_part(k).start()
    keep_part = pltpu.make_async_copy(
        part.at[c, :, pl.ds(pl.multiple_of(y * 128, 128), 128)], got.at[me], pr.at[0])
    keep_part.start()
    keep_part.wait()
    loop(1, 64, lambda k: send_part(k).wait())
    total = lax.fori_loop(0, 64, lambda i, acc: acc + got[i].astype(F32), jnp.zeros((64, 128), F32), unroll=4)
    out[...] = total.T

    loop(1, 16, lambda k: (green1(k).wait_send(), block(k).wait_send()))
    loop(1, 4, lambda k: (green2(k).wait_send(), quarter(k).wait_send()))
    loop(0, 4, lambda k: (green3(k).wait_send(), forward(k).wait_send()))
    loop(1, 64, lambda k: send_w(k).wait_send())


def shards(integrals, virt_green, occ_green, block_list, block_owner, block_sizes):
    dma = pltpu.SemaphoreType.DMA
    vmem = pltpu.VMEM
    return pl.pallas_call(
        kernel,
        out_shape=jax.ShapeDtypeStruct((128, 64), F32),
        in_specs=[SMEM] * 3 + [ANY] * 3,
        out_specs=VMEM,
        scratch_shapes=[
            pltpu.SMEM((128,), jnp.int32),
            pltpu.SMEM((16,), jnp.int32),
            vmem((2, 32, 512), BF),
            vmem((2, 4, 512, 128), BF),
            vmem((16, 8, 32, 256), BF),
            vmem((8, 128, 16, 128), BF),
            vmem((16, 32, 512), BF),
            vmem((16, 32, 512), BF),
            vmem((8, 128, 512), BF),
            vmem((8, 512, 512), BF),
            vmem((16, 8, 32, 256), BF),
            vmem((64, 8, 16, 128), BF),
            vmem((1024, 2048), BF),
            vmem((512, 2048), BF),
            vmem((16, 64, 512), BF),
            vmem((64, 64, 128), BF),
            dma((16,)), dma((16,)), dma((4,)), dma((4,)), dma((4,)), dma((4,)),
            dma((16,)), dma((16,)), dma((4,)), dma((4,)), dma((4,)), dma((4,)),
            dma((64,)), dma((64,)), dma((64,)), dma((64,)), dma((2,)),
        ],
        compiler_params=pltpu.CompilerParams(
            has_side_effects=True, collective_id=0, vmem_limit_bytes=48 << 20),
    )(block_list, block_owner, block_sizes, integrals, virt_green, occ_green)


def solution(mesh):
    in_specs = (P("row", "col", None), P("col", None), P("col", None), P(), P(), P())
    return jax.shard_map(shards, mesh=mesh, in_specs=in_specs, out_specs=P("row", "col"), check_vma=False)
```

```python
import jax
import jax.numpy as jnp
from jax import lax
from jax.experimental import pallas as pl
from jax.experimental.pallas import tpu as pltpu
from jax.sharding import PartitionSpec as P

BF = jnp.bfloat16
F32 = jnp.float32
ANY = pl.BlockSpec(memory_space=pl.ANY)
VMEM = pl.BlockSpec(memory_space=pltpu.VMEM)
SMEM = pl.BlockSpec(memory_space=pltpu.SMEM)
MESH = pl.DeviceIdType.MESH
NT = (((1,), (1,)), ((), ()))
ORDER = (10, 14, 6, 11, 9, 8, 2, 13, 7, 15, 5, 12, 4, 3, 1)


def loop(lo, hi, body, unroll=1):
    def step(i, carry):
        body(i)
        return carry

    lax.fori_loop(lo, hi, step, 0, unroll=unroll)


def remote(src, dst, ssem, rsem, row, col):
    return pltpu.make_async_remote_copy(
        src_ref=src, dst_ref=dst, send_sem=ssem, recv_sem=rsem, device_id=(row, col), device_id_type=MESH,
    )


def arrived(ref, sem):
    pltpu.make_async_copy(ref, ref, sem).wait()


def kernel(lists, owner, sizes, ints, virt, occ, out,
           starts, slot_size, gsrc, green, mine, quart, veff, oeff, left, left_t, wout, wgot, i2, w2, part, got,
           g1s, g1r, g2s, g2r, g3s, g3r, ms, mr, qs, qr, fs, fr, ws, wr, ps, pr, loc):
    r = lax.axis_index("row")
    c = lax.axis_index("col")
    y, core = r // 2, r % 2
    z, x = c // 4, c % 4
    me = y * 16 + c
    twin = y * 2 + (1 - core)

    def col_to(k):
        return (z + k // 4) % 4 * 4 + (x + k % 4) % 4

    def col_from(k):
        return (z + 4 - k // 4) % 4 * 4 + (x + 4 - k % 4) % 4

    def row_to(k):
        return (y + k) % 4 * 2 + core

    def piece(yy):
        return ints.at[:, pl.ds((yy // 2) * 16, 16), pl.ds((yy % 2) * 128, 128)]

    def green1(k):
        src = gsrc.at[core, :, pl.ds(pl.multiple_of(y * 128, 128), 128)]
        return remote(src, green.at[core, y, pl.ds(c * 32, 32)], g1s.at[k], g1r.at[k], r, col_to(k))

    def green2(k):
        return remote(green.at[core, y], green.at[core, y], g2s.at[k], g2r.at[k], row_to(k), c)

    def green3(k):
        q = (y + 4 - k) % 4
        return remote(green.at[core, q], green.at[core, q], g3s.at[k], g3r.at[k], twin, c)

    def block(k):
        return remote(ints.at[pl.ds(col_to(k) * 8, 8)], mine.at[c], ms.at[k], mr.at[k], r, col_to(k))

    def quarter(k):
        return remote(piece((y + k) % 4), quart.at[r], qs.at[k], qr.at[k], row_to(k), c)

    def forward(k):
        frm = (y + 4 - k) % 4 * 2 + core
        return remote(quart.at[frm], quart.at[frm], fs.at[k], fr.at[k], twin, c)

    def send_own():
        return remote(piece(y), quart.at[r], fs.at[0], fr.at[0], twin, c)

    def send_w(k):
        yy, cc = (y + k // 16) % 4, col_to(k % 16)
        return remote(wout.at[cc, yy], wgot.at[me], ws.at[k], wr.at[k], yy * 2 + core, cc)

    def send_part(k):
        yy, cc = (y + k // 16) % 4, col_to(k % 16)
        return remote(part.at[cc, yy], got.at[me], ps.at[k], pr.at[k], yy * 2 + core, cc)

    own = [
        pltpu.make_async_copy(virt, gsrc.at[0], loc.at[0]),
        pltpu.make_async_copy(occ, gsrc.at[1], loc.at[1]),
        pltpu.make_async_copy(ints.at[pl.ds(c * 8, 8)], mine.at[c], mr.at[0]),
        pltpu.make_async_copy(piece(y), quart.at[r], qr.at[0]),
    ]
    for copy in own:
        copy.start()

    barrier = pltpu.get_barrier_semaphore()

    def greet(row, col):
        pl.semaphore_signal(barrier, inc=1, device_id=(row, col), device_id_type=MESH)

    loop(1, 16, lambda k: greet(r, col_to(k)))
    loop(1, 4, lambda k: greet(row_to(k), c))
    greet(twin, c)
    pl.semaphore_wait(barrier, 19)

    own[0].wait()
    own[1].wait()
    keep = pltpu.make_async_copy(
        gsrc.at[core, :, pl.ds(pl.multiple_of(y * 128, 128), 128)], green.at[core, y, pl.ds(c * 32, 32)], g1r.at[0])
    keep.start()
    for k in ORDER:
        green1(k).start()
    for k in ORDER:
        block(k).start()

    for s in range(16):
        atom = jnp.int32(0)
        for a in range(16):
            atom = jnp.where(owner[a] == s, a, atom)
        slot_size[s] = sizes[atom]
        for k in range(8):
            starts[s * 8 + k] = owner[lists[k, atom]]

    keep.wait()
    loop(1, 16, lambda k: green1(k).wait_recv())
    loop(1, 4, lambda k: green2(k).start())
    for k in (2, 1, 3):
        quarter(k).start()
    send_own().start()
    green3(0).start()

    def pass_green(k):
        green2(k).wait_recv()
        green3(k).start()

    loop(1, 4, pass_green)
    loop(0, 4, lambda k: green3(k).wait_recv())

    lane = lax.broadcasted_iota(jnp.int32, (32, 128), 1)
    row = lax.broadcasted_iota(jnp.int32, (32, 128), 0)
    for q in range(4):
        limit = jnp.zeros((32, 128), jnp.int32)
        for s in range(4):
            limit = jnp.where(lane // 32 == s, slot_size[q * 4 + s], limit)
        inside = lane % 32 < limit
        for s in range(16):
            both = jnp.logical_and(inside, row < slot_size[s])
            rows = pl.ds(s * 32, 32)
            veff[s, :, q * 128:(q + 1) * 128] = jnp.where(both, green[0, q, rows, :], jnp.zeros((), BF))
            oeff[s, :, q * 128:(q + 1) * 128] = jnp.where(both, green[1, q, rows, :], jnp.zeros((), BF))

    def listed(ref, s):
        return jnp.concatenate([ref[starts[s * 8 + k]] for k in range(8)], axis=0)

    def make_left(dz):
        zz = (z + 4 - dz) % 4
        for dx in range(4):
            arrived(mine.at[zz * 4 + (x + 4 - dx) % 4], mr.at[dz * 4 + dx])
        for xx in range(4):
            s = zz * 4 + xx
            res = jnp.dot(mine[s].reshape(256, 256), listed(veff, s), preferred_element_type=F32)
            left[:, xx * 32:(xx + 1) * 32, :] = res.astype(BF).reshape(8, 32, 512)
        for p in range(8):
            left_t[p, :, pl.ds(pl.multiple_of(zz * 128, 128), 128)] = left[p].T

    loop(0, 4, make_left)

    def make_w(k):
        t = col_to(k)
        lhs = left_t[:, pl.ds(pl.multiple_of(t * 32, 32), 32), :].reshape(256, 512)
        res = lax.dot_general(lhs, listed(oeff, t), NT, preferred_element_type=F32)
        res = res.astype(BF).reshape(8, 32, 256)
        for q in range(4):
            wout[t, q] = res[:, q // 2 * 16:q // 2 * 16 + 16, q % 2 * 128:q % 2 * 128 + 128]

    for k in ORDER:
        make_w(k)
        for dy in (2, 1, 3, 0):
            send_w(dy * 16 + k).start()
    make_w(0)
    for dy in (2, 1, 3):
        send_w(dy * 16).start()
    keep_w = pltpu.make_async_copy(wout.at[c, y], wgot.at[me], wr.at[0])
    keep_w.start()

    def pass_quarter(k):
        quarter(k).wait_recv()
        forward(k).start()

    loop(1, 4, pass_quarter)
    own[3].wait()

    def lay_i(i):
        v = jnp.swapaxes(quart[i // 8, pl.ds(pl.multiple_of(i % 8 * 16, 16), 16)], 0, 1)
        for j in range(16):
            i2[pl.ds(pl.multiple_of(i * 16, 16), 16), j * 128:(j + 1) * 128] = v[j]

    def lay_piece(rr):
        loop(rr * 8, rr * 8 + 8, lay_i)

    loop(0, 4, lambda k: lay_piece(row_to(k)))

    def lay_other(k):
        forward(k).wait_recv()
        lay_piece((y + 4 - k) % 4 * 2 + 1 - core)

    loop(0, 4, lay_other)

    def lay_w(i):
        yy = (y + 4 - i // 8) % 4
        zz = (z + 4 - i // 2 % 4) % 4
        for h in range(2):
            xx = i % 2 * 2 + h
            k = i // 8 * 16 + i // 2 % 4 * 4 + (x + 4 - xx) % 4
            arrived(wgot.at[yy * 16 + zz * 4 + xx], wr.at[k])
        pair = yy * 8 + zz * 2 + i % 2
        v = jnp.swapaxes(wgot[pl.ds(pair * 2, 2)].reshape(16, 16, 128), 0, 1)
        for j in range(16):
            w2[pl.ds(pl.multiple_of(pair * 16, 16), 16), j * 128:(j + 1) * 128] = v[j]

    loop(0, 32, lay_w)

    def multiply(dz):
        zz = (z + dz) % 4
        v = i2[pl.ds(pl.multiple_of(zz * 256, 256), 256), :]
        res = lax.dot_general(v, w2[...], NT, preferred_element_type=F32)
        res = res.astype(BF).reshape(4, 64, 512)
        for q in range(4):
            part[pl.ds(zz * 4, 4), q] = res[:, :, q * 128:(q + 1) * 128]

    for group in ((2,), (1, 3), (0,)):
        for dz in group:
            multiply(dz)
        for dx in (2, 1, 3, 0):
            for dy in (2, 1, 3, 0):
                for dz in group:
                    k = dy * 16 + dz * 4 + dx
                    if k:
                        send_part(k).start()
    keep_part = pltpu.make_async_copy(part.at[c, y], got.at[me], pr.at[0])
    keep_part.start()
    keep_part.wait()
    loop(1, 64, lambda k: send_part(k).wait())
    total = lax.fori_loop(0, 64, lambda i, acc: acc + got[i].astype(F32), jnp.zeros((64, 128), F32), unroll=4)
    out[...] = total

    loop(1, 16, lambda k: (green1(k).wait_send(), block(k).wait_send()))
    loop(1, 4, lambda k: (green2(k).wait_send(), quarter(k).wait_send()))
    loop(0, 4, lambda k: (green3(k).wait_send(), forward(k).wait_send()))
    loop(1, 64, lambda k: send_w(k).wait_send())


def shards(integrals, virt_green, occ_green, block_list, block_owner, block_sizes):
    dma = pltpu.SemaphoreType.DMA
    vmem = pltpu.VMEM
    res = pl.pallas_call(
        kernel,
        out_shape=jax.ShapeDtypeStruct((64, 128), F32),
        in_specs=[SMEM] * 3 + [ANY] * 3,
        out_specs=VMEM,
        scratch_shapes=[
            pltpu.SMEM((128,), jnp.int32),
            pltpu.SMEM((16,), jnp.int32),
            vmem((2, 32, 512), BF),
            vmem((2, 4, 512, 128), BF),
            vmem((16, 8, 32, 256), BF),
            vmem((8, 128, 16, 128), BF),
            vmem((16, 32, 512), BF),
            vmem((16, 32, 512), BF),
            vmem((8, 128, 512), BF),
            vmem((8, 512, 512), BF),
            vmem((16, 4, 8, 16, 128), BF),
            vmem((64, 8, 16, 128), BF),
            vmem((1024, 2048), BF),
            vmem((512, 2048), BF),
            vmem((16, 4, 64, 128), BF),
            vmem((64, 64, 128), BF),
            dma((16,)), dma((16,)), dma((4,)), dma((4,)), dma((4,)), dma((4,)),
            dma((16,)), dma((16,)), dma((4,)), dma((4,)), dma((4,)), dma((4,)),
            dma((64,)), dma((64,)), dma((64,)), dma((64,)), dma((2,)),
        ],
        compiler_params=pltpu.CompilerParams(
            has_side_effects=True, collective_id=0, vmem_limit_bytes=63 << 20),
    )(block_list.T, block_owner, block_sizes, integrals, virt_green, occ_green)
    return res.T


def solution(mesh):
    in_specs = (P("row", "col", None), P("col", None), P("col", None), P(), P(), P())
    return jax.shard_map(shards, mesh=mesh, in_specs=in_specs, out_specs=P("row", "col"), check_vma=False)
```

```python
import jax
import jax.numpy as jnp
from jax import lax
from jax.experimental import pallas as pl
from jax.experimental.pallas import tpu as pltpu
from jax.sharding import PartitionSpec as P

BF = jnp.bfloat16
F32 = jnp.float32
ANY = pl.BlockSpec(memory_space=pl.ANY)
VMEM = pl.BlockSpec(memory_space=pltpu.VMEM)
SMEM = pl.BlockSpec(memory_space=pltpu.SMEM)
MESH = pl.DeviceIdType.MESH
NT = (((1,), (1,)), ((), ()))
ORDER = (10, 14, 6, 11, 9, 8, 2, 13, 7, 15, 5, 12, 4, 3, 1)


def loop(lo, hi, body, unroll=1):
    def step(i, carry):
        body(i)
        return carry

    lax.fori_loop(lo, hi, step, 0, unroll=unroll)


def remote(src, dst, ssem, rsem, row, col):
    return pltpu.make_async_remote_copy(
        src_ref=src, dst_ref=dst, send_sem=ssem, recv_sem=rsem, device_id=(row, col), device_id_type=MESH,
    )


def arrived(ref, sem):
    pltpu.make_async_copy(ref, ref, sem).wait()


def kernel(lists_in, owner_in, sizes_in, ints, virt, occ, out,
           lists, owner, sizes, starts, slot_size, vall, oall, mine, quart, veff, oeff, left, left_t, wout, wgot, i2, w2, half0, part, got,
           loc, v1s, v1r, v2s, v2r, o1s, o1r, o2s, o2r, ms, mr, qs, qr, fs, fr, ws, wr, ps, pr):
    r = lax.axis_index("row")
    c = lax.axis_index("col")
    y, core = r >> 1, r & 1
    z, x = c >> 2, c & 3
    me = y * 16 + c
    twin = y * 2 + (1 - core)

    cols = [((z + k // 4) & 3) * 4 + ((x + k % 4) & 3) for k in range(16)]
    ys = [(y + k) & 3 for k in range(4)]

    def col_to(k):
        return cols[k] if isinstance(k, int) else ((z + (k >> 2)) & 3) * 4 + ((x + (k & 3)) & 3)

    def y_to(k):
        return ys[k] if isinstance(k, int) else (y + k) & 3

    def row_to(k):
        return y_to(k) * 2 + core

    def piece(yy, u):
        return ints.at[pl.ds(u * 64, 64), pl.ds((yy >> 1) * 16, 16), pl.ds((yy & 1) * 128, 128)]

    half_rows = pl.ds(core * 16, 16)

    def virt1(k):
        return remote(virt.at[half_rows], vall.at[c, half_rows], v1s.at[k], v1r.at[k], r, col_to(k))

    def virt2():
        part = vall.at[:, half_rows]
        return remote(part, part, v2s.at[0], v2r.at[0], twin, c)

    def occ1(k):
        return remote(occ.at[half_rows], oall.at[c, half_rows], o1s.at[k], o1r.at[k], r, col_to(k))

    def occ2():
        part = oall.at[:, half_rows]
        return remote(part, part, o2s.at[0], o2r.at[0], twin, c)

    def block(h, k):
        src = ints.at[pl.ds(h * 64 + col_to(k) * 4, 4)]
        return remote(src, mine.at[h, c], ms.at[h * 16 + k], mr.at[h * 16 + k], r, col_to(k))

    def quarter(u, k):
        dst = quart.at[r, pl.ds(u * 64, 64)]
        return remote(piece(y_to(k), u), dst, qs.at[u * 4 + k], qr.at[u * 4 + k], row_to(k), c)

    def forward(u, k):
        part = quart.at[((y - k) & 3) * 2 + core, pl.ds(u * 64, 64)]
        return remote(part, part, fs.at[u * 4 + k], fr.at[u * 4 + k], twin, c)

    def send_own(u):
        dst = quart.at[r, pl.ds(u * 64, 64)]
        return remote(piece(y, u), dst, fs.at[u * 4], fr.at[u * 4], twin, c)

    def send_w(h, k):
        yy, cc = y_to(k >> 4), col_to(k & 15)
        at = h * 64 + k
        return remote(wout.at[h, cc, yy], wgot.at[h, me], ws.at[at], wr.at[at], yy * 2 + core, cc)

    def send_part(k):
        yy, cc = y_to(k >> 4), col_to(k & 15)
        return remote(part.at[cc, yy], got.at[me], ps.at[0], pr.at[0], yy * 2 + core, cc)

    tables = [
        pltpu.make_async_copy(src, dst, loc.at[i])
        for i, (src, dst) in enumerate(((lists_in, lists), (owner_in, owner), (sizes_in, sizes)))
    ]
    own = [
        pltpu.make_async_copy(virt.at[half_rows], vall.at[c, half_rows], v1r.at[0]),
        pltpu.make_async_copy(occ.at[half_rows], oall.at[c, half_rows], o1r.at[0]),
        pltpu.make_async_copy(ints.at[pl.ds(c * 4, 4)], mine.at[0, c], mr.at[0]),
        pltpu.make_async_copy(ints.at[pl.ds(64 + c * 4, 4)], mine.at[1, c], mr.at[16]),
        pltpu.make_async_copy(piece(y, 0), quart.at[r, pl.ds(0, 64)], qr.at[0]),
        pltpu.make_async_copy(piece(y, 1), quart.at[r, pl.ds(64, 64)], qr.at[4]),
    ]
    for copy in tables + own:
        copy.start()

    barrier = pltpu.get_barrier_semaphore()

    def greet(row, col):
        pl.semaphore_signal(barrier, inc=1, device_id=(row, col), device_id_type=MESH)

    loop(1, 16, lambda k: greet(r, col_to(k)))
    loop(1, 4, lambda k: greet(row_to(k), c))
    greet(twin, c)

    pl.semaphore_wait(barrier, 19)
    for k in (2, 1, 3):
        quarter(0, k).start()
    for k in ORDER:
        virt1(k).start()
    for k in ORDER:
        occ1(k).start()
    for k in ORDER:
        block(0, k).start()
    send_own(0).start()

    for copy in tables:
        copy.wait()
    for s in range(16):
        atom = jnp.int32(0)
        for a in range(16):
            atom = jnp.where(owner[a] == s, a, atom)
        slot_size[s] = sizes[atom]
        for k in range(8):
            starts[s * 8 + k] = owner[lists[k, atom]]

    own[0].wait()
    loop(1, 16, lambda k: virt1(k).wait_recv())
    virt2().start()
    own[1].wait()
    loop(1, 16, lambda k: occ1(k).wait_recv())
    occ2().start()
    for i, k in enumerate(ORDER):
        block(1, k).start()
        if i % 5 == 1:
            quarter(1, (2, 1, 3)[i // 5]).start()
    send_own(1).start()
    virt2().wait_recv()

    lane = lax.broadcasted_iota(jnp.int32, (32, 512), 1)
    row = lax.broadcasted_iota(jnp.int32, (32, 512), 0)
    limit = jnp.zeros((32, 512), jnp.int32)
    for s in range(16):
        limit = jnp.where(lane // 32 == s, slot_size[s], limit)
    inside = lane % 32 < limit

    def mask(ref, dst):
        def one(s):
            both = jnp.logical_and(inside, row < slot_size[s])
            dst[s] = jnp.where(both, ref[s], jnp.zeros((), BF))

        loop(0, 16, one, 4)

    mask(vall, veff)

    def listed(ref, s):
        return jnp.concatenate([ref[starts[s * 8 + k]] for k in range(8)], axis=0)

    def make_left(h, i):
        dz = (2 + i) & 3
        zz = ((z - dz) & 3)
        for dx in range(4):
            arrived(mine.at[h, zz * 4 + ((x - dx) & 3)], mr.at[h * 16 + dz * 4 + dx])
        for xx in range(4):
            s = zz * 4 + xx
            res = jnp.dot(mine[h, s].reshape(128, 256), listed(veff, s), preferred_element_type=F32)
            left[:, xx * 32:(xx + 1) * 32, :] = res.astype(BF).reshape(4, 32, 512)
        for p in range(4):
            left_t[p, :, pl.ds(pl.multiple_of(zz * 128, 128), 128)] = left[p].T

    def make_w(h, k):
        t = col_to(k)
        lhs = left_t[:, pl.ds(pl.multiple_of(t * 32, 32), 32), :].reshape(128, 512)
        res = lax.dot_general(lhs, listed(oeff, t), NT, preferred_element_type=F32)
        res = res.astype(BF).reshape(4, 32, 256)
        for q in range(4):
            wout[h, t, q] = res[:, q // 2 * 16:q // 2 * 16 + 16, q % 2 * 128:q % 2 * 128 + 128]

    def pass_quarter(u):
        def one(k):
            quarter(u, k).wait_recv()
            forward(u, k).start()

        loop(1, 4, one)
        own[4 + u].wait()

    def lay_i(i):
        v = jnp.swapaxes(quart[i // 8, pl.ds(pl.multiple_of(i % 8 * 16, 16), 16)], 0, 1)
        for j in range(16):
            i2[pl.ds(pl.multiple_of(i * 16, 16), 16), j * 128:(j + 1) * 128] = v[j]

    def lay_piece(u, rr):
        loop(rr * 8 + u * 4, rr * 8 + u * 4 + 4, lay_i)

    def half(h):
        @pl.when(h == 1)
        def _():
            pass_quarter(0)
            loop(0, 4, lambda k: lay_piece(0, row_to(k)))

        loop(0, 4, lambda i: make_left(h, i))

        @pl.when(h == 0)
        def _():
            occ2().wait_recv()
            mask(oall, oeff)

        for k in ORDER:
            make_w(h, k)
            for dy in (2, 1, 3, 0):
                send_w(h, dy * 16 + k).start()
        make_w(h, 0)
        for dy in (2, 1, 3):
            send_w(h, dy * 16).start()
        pltpu.make_async_copy(wout.at[h, c, y], wgot.at[h, me], wr.at[h * 64]).start()

    loop(0, 2, half)

    pass_quarter(1)

    def lay_other(u, k):
        forward(u, k).wait_recv()
        lay_piece(u, ((y - k) & 3) * 2 + 1 - core)

    loop(0, 4, lambda k: lay_other(0, k))
    loop(0, 4, lambda k: lay_piece(1, row_to(k)))
    loop(0, 4, lambda k: lay_other(1, k))

    def lay_w(h, i):
        dy, dz = i // 4, i % 4
        yy = ((y - dy) & 3)
        first = yy * 16 + ((z - dz) & 3) * 4
        for dx in range(4):
            arrived(wgot.at[h, first + ((x - dx) & 3)], wr.at[h * 64 + dy * 16 + dz * 4 + dx])
        v = jnp.swapaxes(wgot[h, pl.ds(first, 4)].reshape(16, 16, 128), 0, 1)
        at = (yy + h * (1 - 2 * (yy % 2))) * 64 + first % 16 * 4
        for j in range(16):
            w2[h, pl.ds(pl.multiple_of(at, 16), 16), j * 128:(j + 1) * 128] = v[j]

    def product(h, at, size):
        v = i2[pl.ds(pl.multiple_of(at, size), size), :]
        return lax.dot_general(v, w2[h], NT, preferred_element_type=F32).astype(BF)

    def multiply0(i):
        half0[pl.ds(pl.multiple_of(i * 512, 512), 512), :] = product(0, i * 512, 512)

    low = lax.broadcasted_iota(jnp.int32, (256, 128), 1) < 64

    def multiply1(dz):
        zz = (z + dz) & 3
        res = product(1, zz * 256, 256)
        old = half0[pl.ds(pl.multiple_of(zz * 256, 256), 256), :]
        for q in range(2):
            one, two = old[:, q * 128:(q + 1) * 128], res[:, q * 128:(q + 1) * 128]
            part[pl.ds(zz * 4, 4), q * 2] = jnp.where(low, one, two).reshape(4, 64, 128)
            part[pl.ds(zz * 4, 4), q * 2 + 1] = jnp.where(low, two, one).reshape(4, 64, 128)

    loop(0, 16, lambda i: lay_w(0, i))
    loop(0, 2, multiply0)
    loop(0, 16, lambda i: lay_w(1, i))
    for group in ((2,), (1, 3), (0,)):
        for dz in group:
            multiply1(dz)
        for dx in (2, 1, 3, 0):
            for dy in (2, 1, 3, 0):
                for dz in group:
                    k = dy * 16 + dz * 4 + dx
                    if k:
                        send_part(k).start()
    pltpu.make_async_copy(part.at[c, y], got.at[me], pr.at[0]).start()

    loop(1, 16, lambda k: (virt1(k).wait_send(), occ1(k).wait_send()))
    loop(1, 16, lambda k: (block(0, k).wait_send(), block(1, k).wait_send()))
    loop(1, 4, lambda k: (quarter(0, k).wait_send(), quarter(1, k).wait_send()))
    virt2().wait_send()
    occ2().wait_send()
    loop(0, 4, lambda k: (forward(0, k).wait_send(), forward(1, k).wait_send()))
    loop(1, 64, lambda k: (send_w(0, k).wait_send(), send_w(1, k).wait_send()))
    arrived(got, pr.at[0])
    total = lax.fori_loop(0, 64, lambda i, acc: acc + got[i].astype(F32), jnp.zeros((64, 128), F32), unroll=4)
    out[...] = jnp.where((y & 1) == 1, pltpu.roll(total, 64, 1), total)

    arrived(got.at[pl.ds(0, 63)], ps.at[0])


def shards(integrals, virt_green, occ_green, block_list, block_owner, block_sizes):
    dma = pltpu.SemaphoreType.DMA
    vmem = pltpu.VMEM
    res = pl.pallas_call(
        kernel,
        out_shape=jax.ShapeDtypeStruct((64, 128), F32),
        in_specs=[ANY] * 6,
        out_specs=VMEM,
        scratch_shapes=[
            pltpu.SMEM((8, 16), jnp.int32),
            pltpu.SMEM((16,), jnp.int32),
            pltpu.SMEM((16,), jnp.int32),
            pltpu.SMEM((128,), jnp.int32),
            pltpu.SMEM((16,), jnp.int32),
            vmem((16, 32, 512), BF),
            vmem((16, 32, 512), BF),
            vmem((2, 16, 4, 32, 256), BF),
            vmem((8, 128, 16, 128), BF),
            vmem((16, 32, 512), BF),
            vmem((16, 32, 512), BF),
            vmem((4, 128, 512), BF),
            vmem((4, 512, 512), BF),
            vmem((2, 16, 4, 4, 16, 128), BF),
            vmem((2, 64, 4, 16, 128), BF),
            vmem((1024, 2048), BF),
            vmem((2, 256, 2048), BF),
            vmem((1024, 256), BF),
            vmem((16, 4, 64, 128), BF),
            vmem((64, 64, 128), BF),
            dma((3,)), dma((16,)), dma((16,)), dma((1,)), dma((1,)),
            dma((16,)), dma((16,)), dma((1,)), dma((1,)),
            dma((32,)), dma((32,)), dma((8,)), dma((8,)), dma((8,)), dma((8,)),
            dma((128,)), dma((128,)), dma((1,)), dma((1,)),
        ],
        compiler_params=pltpu.CompilerParams(
            has_side_effects=True, collective_id=0, vmem_limit_bytes=63 << 20),
    )(block_list.T, block_owner, block_sizes, integrals, virt_green, occ_green)
    return res.T


def solution(mesh):
    in_specs = (P("row", "col", None), P("col", None), P("col", None), P(), P(), P())
    return jax.shard_map(shards, mesh=mesh, in_specs=in_specs, out_specs=P("row", "col"), check_vma=False)
```

```python
import jax
import jax.numpy as jnp
from jax import lax
from jax.experimental import pallas as pl
from jax.experimental.pallas import tpu as pltpu
from jax.sharding import PartitionSpec as P

BF = jnp.bfloat16
F32 = jnp.float32
ANY = pl.BlockSpec(memory_space=pl.ANY)
VMEM = pl.BlockSpec(memory_space=pltpu.VMEM)
SMEM = pl.BlockSpec(memory_space=pltpu.SMEM)
MESH = pl.DeviceIdType.MESH
NT = (((1,), (1,)), ((), ()))
ORDER = (10, 14, 6, 11, 9, 8, 2, 13, 7, 15, 5, 12, 4, 3, 1)
MIXED = (10, 1, 14, 4, 6, 3, 11, 12, 9, 2, 8, 5, 7, 13, 15, 0)


def loop(lo, hi, body, unroll=1):
    def step(i, carry):
        body(i)
        return carry

    lax.fori_loop(lo, hi, step, 0, unroll=unroll)


def remote(src, dst, ssem, rsem, row, col):
    return pltpu.make_async_remote_copy(
        src_ref=src, dst_ref=dst, send_sem=ssem, recv_sem=rsem, device_id=(row, col), device_id_type=MESH,
    )


def arrived(ref, sem):
    pltpu.make_async_copy(ref, ref, sem).wait()


def kernel(lists_in, owner_in, sizes_in, ints, virt, occ, out,
           lists, owner, sizes, starts, slot_size, vall, oall, mine, quart, veff, oeff, left, left_t, wout, wgot, i2, w2, half0, part, got,
           loc, v1s, v1r, v2s, v2r, o1s, o1r, o2s, o2r, ms, mr, qs, qr, fs, fr, ws, wr, ps, pr):
    r = lax.axis_index("row")
    c = lax.axis_index("col")
    y, core = r >> 1, r & 1
    z, x = c >> 2, c & 3
    me = y * 16 + c
    twin = y * 2 + (1 - core)

    cols = [((z + k // 4) & 3) * 4 + ((x + k % 4) & 3) for k in range(16)]
    ys = [(y + k) & 3 for k in range(4)]

    def col_to(k):
        return cols[k] if isinstance(k, int) else ((z + (k >> 2)) & 3) * 4 + ((x + (k & 3)) & 3)

    def y_to(k):
        return ys[k] if isinstance(k, int) else (y + k) & 3

    def row_to(k):
        return y_to(k) * 2 + core

    def piece(yy, u):
        return ints.at[pl.ds(u * 64, 64), pl.ds((yy >> 1) * 16, 16), pl.ds((yy & 1) * 128, 128)]

    half_rows = pl.ds(core * 16, 16)

    def virt1(k):
        return remote(virt.at[half_rows], vall.at[c, half_rows], v1s.at[k], v1r.at[k], r, col_to(k))

    def virt2():
        part = vall.at[:, half_rows]
        return remote(part, part, v2s.at[0], v2r.at[0], twin, c)

    def occ1(k):
        return remote(occ.at[half_rows], oall.at[c, half_rows], o1s.at[k], o1r.at[k], r, col_to(k))

    def occ2():
        part = oall.at[:, half_rows]
        return remote(part, part, o2s.at[0], o2r.at[0], twin, c)

    def block(h, k):
        src = ints.at[pl.ds(h * 64 + col_to(k) * 4, 4)]
        return remote(src, mine.at[h, c], ms.at[h * 16 + k], mr.at[h * 16 + k], r, col_to(k))

    def quarter(u, k):
        dst = quart.at[r, pl.ds(u * 64, 64)]
        return remote(piece(y_to(k), u), dst, qs.at[u * 4 + k], qr.at[u * 4 + k], row_to(k), c)

    def forward(u, k):
        part = quart.at[((y - k) & 3) * 2 + core, pl.ds(u * 64, 64)]
        return remote(part, part, fs.at[u * 4 + k], fr.at[u * 4 + k], twin, c)

    def send_own(u):
        dst = quart.at[r, pl.ds(u * 64, 64)]
        return remote(piece(y, u), dst, fs.at[u * 4], fr.at[u * 4], twin, c)

    def send_w(h, k):
        yy, cc = y_to(k >> 4), col_to(k & 15)
        at = h * 64 + k
        return remote(wout.at[h, cc, yy], wgot.at[h, me], ws.at[at], wr.at[at], yy * 2 + core, cc)

    def send_part(k):
        yy, cc = y_to(k >> 4), col_to(k & 15)
        return remote(part.at[cc, yy], got.at[me], ps.at[0], pr.at[0], yy * 2 + core, cc)

    tables = [
        pltpu.make_async_copy(src, dst, loc.at[i])
        for i, (src, dst) in enumerate(((lists_in, lists), (owner_in, owner), (sizes_in, sizes)))
    ]
    own = [
        pltpu.make_async_copy(virt.at[half_rows], vall.at[c, half_rows], v1r.at[0]),
        pltpu.make_async_copy(occ.at[half_rows], oall.at[c, half_rows], o1r.at[0]),
        pltpu.make_async_copy(ints.at[pl.ds(c * 4, 4)], mine.at[0, c], mr.at[0]),
        pltpu.make_async_copy(ints.at[pl.ds(64 + c * 4, 4)], mine.at[1, c], mr.at[16]),
        pltpu.make_async_copy(piece(y, 0), quart.at[r, pl.ds(0, 64)], qr.at[0]),
        pltpu.make_async_copy(piece(y, 1), quart.at[r, pl.ds(64, 64)], qr.at[4]),
    ]
    for copy in tables + own:
        copy.start()

    barrier = pltpu.get_barrier_semaphore()

    def greet(row, col):
        pl.semaphore_signal(barrier, inc=1, device_id=(row, col), device_id_type=MESH)

    loop(1, 16, lambda k: greet(r, col_to(k)))
    loop(1, 4, lambda k: greet(row_to(k), c))
    greet(twin, c)

    pl.semaphore_wait(barrier, 19)
    for k in (2, 1, 3):
        quarter(0, k).start()
    for k in ORDER:
        virt1(k).start()
    for k in ORDER:
        occ1(k).start()
    for k in ORDER:
        block(0, k).start()
    send_own(0).start()

    for copy in tables:
        copy.wait()
    for s in range(16):
        atom = jnp.int32(0)
        for a in range(16):
            atom = jnp.where(owner[a] == s, a, atom)
        slot_size[s] = sizes[atom]
        for k in range(8):
            starts[s * 8 + k] = owner[lists[k, atom]]

    own[0].wait()
    loop(1, 16, lambda k: virt1(k).wait_recv())
    virt2().start()
    own[1].wait()
    loop(1, 16, lambda k: occ1(k).wait_recv())
    occ2().start()
    for k in (2, 1, 3):
        quarter(1, k).start()
    send_own(1).start()

    def second(k):
        block(0, k).wait_send()
        block(1, k).start()

    for k in ORDER[:8]:
        second(k)
    virt2().wait_recv()

    lane = lax.broadcasted_iota(jnp.int32, (32, 512), 1)
    row = lax.broadcasted_iota(jnp.int32, (32, 512), 0)
    limit = jnp.zeros((32, 512), jnp.int32)
    for s in range(16):
        limit = jnp.where(lane // 32 == s, slot_size[s], limit)
    inside = lane % 32 < limit

    def mask(ref, dst):
        def one(s):
            both = jnp.logical_and(inside, row < slot_size[s])
            dst[s] = jnp.where(both, ref[s], jnp.zeros((), BF))

        loop(0, 16, one, 4)

    mask(vall, veff)
    for k in ORDER[8:]:
        second(k)

    def listed(ref, s):
        return jnp.concatenate([ref[starts[s * 8 + k]] for k in range(8)], axis=0)

    def make_left(h, i):
        dz = (2 + i) & 3
        zz = ((z - dz) & 3)
        for dx in range(4):
            arrived(mine.at[h, zz * 4 + ((x - dx) & 3)], mr.at[h * 16 + dz * 4 + dx])
        for xx in range(4):
            s = zz * 4 + xx
            res = jnp.dot(mine[h, s].reshape(128, 256), listed(veff, s), preferred_element_type=F32)
            left[:, xx * 32:(xx + 1) * 32, :] = res.astype(BF).reshape(4, 32, 512)
        for p in range(4):
            left_t[p, :, pl.ds(pl.multiple_of(zz * 128, 128), 128)] = left[p].T

    def make_w(h, k):
        t = col_to(k)
        lhs = left_t[:, pl.ds(pl.multiple_of(t * 32, 32), 32), :].reshape(128, 512)
        res = lax.dot_general(lhs, listed(oeff, t), NT, preferred_element_type=F32)
        res = res.astype(BF).reshape(4, 32, 256)
        for q in range(4):
            wout[h, t, q] = res[:, q // 2 * 16:q // 2 * 16 + 16, q % 2 * 128:q % 2 * 128 + 128]

    def pass_quarter(u):
        def one(k):
            quarter(u, k).wait_recv()
            forward(u, k).start()

        loop(1, 4, one)
        own[4 + u].wait()

    def lay_i(i):
        v = jnp.swapaxes(quart[i // 8, pl.ds(pl.multiple_of(i % 8 * 16, 16), 16)], 0, 1)
        for j in range(16):
            i2[pl.ds(pl.multiple_of(i * 16, 16), 16), j * 128:(j + 1) * 128] = v[j]

    def lay_piece(u, rr):
        loop(rr * 8 + u * 4, rr * 8 + u * 4 + 4, lay_i)

    def half(h):
        loop(0, 4, lambda i: make_left(h, i))

        @pl.when(h == 0)
        def _():
            occ2().wait_recv()
            mask(oall, oeff)

        for g in range(0, 16, 4):
            for k in MIXED[g:g + 4]:
                make_w(h, k)
            for k in MIXED[g:g + 4]:
                for dy in (2, 1, 3, 0):
                    if dy * 16 + k:
                        send_w(h, dy * 16 + k).start()
        pltpu.make_async_copy(wout.at[h, c, y], wgot.at[h, me], wr.at[h * 64]).start()

    loop(0, 2, half)

    pass_quarter(0)
    pass_quarter(1)

    def lay_other(u, k):
        forward(u, k).wait_recv()
        lay_piece(u, ((y - k) & 3) * 2 + 1 - core)

    loop(0, 4, lambda k: lay_piece(0, row_to(k)))
    loop(0, 4, lambda k: lay_piece(1, row_to(k)))
    loop(0, 4, lambda k: lay_other(0, k))
    loop(0, 4, lambda k: lay_other(1, k))

    def lay_w(h, i):
        dy, dz = i // 4, i % 4
        yy = ((y - dy) & 3)
        first = yy * 16 + ((z - dz) & 3) * 4
        for dx in range(4):
            arrived(wgot.at[h, first + ((x - dx) & 3)], wr.at[h * 64 + dy * 16 + dz * 4 + dx])
        v = jnp.swapaxes(wgot[h, pl.ds(first, 4)].reshape(16, 16, 128), 0, 1)
        at = (yy + h * (1 - 2 * (yy % 2))) * 64 + first % 16 * 4
        for j in range(16):
            w2[h, pl.ds(pl.multiple_of(at, 16), 16), j * 128:(j + 1) * 128] = v[j]

    def product(h, at, size):
        v = i2[pl.ds(pl.multiple_of(at, size), size), :]
        return lax.dot_general(v, w2[h], NT, preferred_element_type=F32).astype(BF)

    def multiply0(i):
        half0[pl.ds(pl.multiple_of(i * 512, 512), 512), :] = product(0, i * 512, 512)

    low = lax.broadcasted_iota(jnp.int32, (256, 128), 1) < 64

    def multiply1(dz):
        zz = (z + dz) & 3
        res = product(1, zz * 256, 256)
        old = half0[pl.ds(pl.multiple_of(zz * 256, 256), 256), :]
        for q in range(2):
            one, two = old[:, q * 128:(q + 1) * 128], res[:, q * 128:(q + 1) * 128]
            part[pl.ds(zz * 4, 4), q * 2] = jnp.where(low, one, two).reshape(4, 64, 128)
            part[pl.ds(zz * 4, 4), q * 2 + 1] = jnp.where(low, two, one).reshape(4, 64, 128)

    loop(0, 16, lambda i: lay_w(0, i))
    loop(0, 2, multiply0)
    loop(0, 16, lambda i: lay_w(1, i))
    for group in ((2,), (1, 3), (0,)):
        for dz in group:
            multiply1(dz)
        for dx in (2, 1, 3, 0):
            for dy in (2, 1, 3, 0):
                for dz in group:
                    k = dy * 16 + dz * 4 + dx
                    if k:
                        send_part(k).start()
    pltpu.make_async_copy(part.at[c, y], got.at[me], pr.at[0]).start()

    loop(1, 16, lambda k: (virt1(k).wait_send(), occ1(k).wait_send()))
    loop(1, 16, lambda k: block(1, k).wait_send())
    loop(1, 4, lambda k: (quarter(0, k).wait_send(), quarter(1, k).wait_send()))
    virt2().wait_send()
    occ2().wait_send()
    loop(0, 4, lambda k: (forward(0, k).wait_send(), forward(1, k).wait_send()))
    loop(1, 64, lambda k: (send_w(0, k).wait_send(), send_w(1, k).wait_send()))
    arrived(got, pr.at[0])
    total = lax.fori_loop(0, 64, lambda i, acc: acc + got[i].astype(F32), jnp.zeros((64, 128), F32), unroll=4)
    out[...] = jnp.where((y & 1) == 1, pltpu.roll(total, 64, 1), total)

    arrived(got.at[pl.ds(0, 63)], ps.at[0])


def shards(integrals, virt_green, occ_green, block_list, block_owner, block_sizes):
    dma = pltpu.SemaphoreType.DMA
    vmem = pltpu.VMEM
    res = pl.pallas_call(
        kernel,
        out_shape=jax.ShapeDtypeStruct((64, 128), F32),
        in_specs=[ANY] * 6,
        out_specs=VMEM,
        scratch_shapes=[
            pltpu.SMEM((8, 16), jnp.int32),
            pltpu.SMEM((16,), jnp.int32),
            pltpu.SMEM((16,), jnp.int32),
            pltpu.SMEM((128,), jnp.int32),
            pltpu.SMEM((16,), jnp.int32),
            vmem((16, 32, 512), BF),
            vmem((16, 32, 512), BF),
            vmem((2, 16, 4, 32, 256), BF),
            vmem((8, 128, 16, 128), BF),
            vmem((16, 32, 512), BF),
            vmem((16, 32, 512), BF),
            vmem((4, 128, 512), BF),
            vmem((4, 512, 512), BF),
            vmem((2, 16, 4, 4, 16, 128), BF),
            vmem((2, 64, 4, 16, 128), BF),
            vmem((1024, 2048), BF),
            vmem((2, 256, 2048), BF),
            vmem((1024, 256), BF),
            vmem((16, 4, 64, 128), BF),
            vmem((64, 64, 128), BF),
            dma((3,)), dma((16,)), dma((16,)), dma((1,)), dma((1,)),
            dma((16,)), dma((16,)), dma((1,)), dma((1,)),
            dma((32,)), dma((32,)), dma((8,)), dma((8,)), dma((8,)), dma((8,)),
            dma((128,)), dma((128,)), dma((1,)), dma((1,)),
        ],
        compiler_params=pltpu.CompilerParams(
            has_side_effects=True, collective_id=0, vmem_limit_bytes=63 << 20),
    )(block_list.T, block_owner, block_sizes, integrals, virt_green, occ_green)
    return res.T


def solution(mesh):
    in_specs = (P("row", "col", None), P("col", None), P("col", None), P(), P(), P())
    return jax.shard_map(shards, mesh=mesh, in_specs=in_specs, out_specs=P("row", "col"), check_vma=False)
```

```python
import jax
import jax.numpy as jnp
from jax import lax
from jax.experimental import pallas as pl
from jax.experimental.pallas import tpu as pltpu
from jax.sharding import PartitionSpec as P

BF = jnp.bfloat16
F32 = jnp.float32
ANY = pl.BlockSpec(memory_space=pl.ANY)
VMEM = pl.BlockSpec(memory_space=pltpu.VMEM)
SMEM = pl.BlockSpec(memory_space=pltpu.SMEM)
MESH = pl.DeviceIdType.MESH
NT = (((1,), (1,)), ((), ()))
ORDER = (10, 14, 6, 11, 9, 8, 2, 13, 7, 15, 5, 12, 4, 3, 1)
MIXED = (10, 1, 14, 4, 6, 3, 11, 12, 9, 2, 8, 5, 7, 13, 15, 0)


def loop(lo, hi, body, unroll=1):
    def step(i, carry):
        body(i)
        return carry

    lax.fori_loop(lo, hi, step, 0, unroll=unroll)


def remote(src, dst, ssem, rsem, row, col):
    return pltpu.make_async_remote_copy(
        src_ref=src, dst_ref=dst, send_sem=ssem, recv_sem=rsem, device_id=(row, col), device_id_type=MESH,
    )


def arrived(ref, sem):
    pltpu.make_async_copy(ref, ref, sem).wait()


def kernel(lists_in, owner_in, sizes_in, ints, virt, occ, out,
           lists, owner, sizes, starts, slot_size, vall, oall, mine, quart, veff, oeff, left, left_t, wout, wgot, i2, w2, half0, part, got,
           loc, v1s, v1r, v2s, v2r, o1s, o1r, o2s, o2r, o3s, o3r, ms, mr, qs, qr, fs, fr, ws, wr, ps, pr):
    r = lax.axis_index("row")
    c = lax.axis_index("col")
    y, core = r >> 1, r & 1
    z, x = c >> 2, c & 3
    me = y * 16 + c
    twin = y * 2 + (1 - core)

    cols = [((z + k // 4) & 3) * 4 + ((x + k % 4) & 3) for k in range(16)]
    ys = [(y + k) & 3 for k in range(4)]

    def col_to(k):
        return cols[k] if isinstance(k, int) else ((z + (k >> 2)) & 3) * 4 + ((x + (k & 3)) & 3)

    def y_to(k):
        return ys[k] if isinstance(k, int) else (y + k) & 3

    def row_to(k):
        return y_to(k) * 2 + core

    def piece(yy, u):
        return ints.at[pl.ds(u * 64, 64), pl.ds((yy >> 1) * 16, 16), pl.ds((yy & 1) * 128, 128)]

    half_rows = pl.ds(core * 16, 16)

    def virt1(k):
        return remote(virt.at[half_rows], vall.at[c, half_rows], v1s.at[k], v1r.at[k], r, col_to(k))

    def virt2():
        part = vall.at[:, half_rows]
        return remote(part, part, v2s.at[0], v2r.at[0], twin, c)

    occ_piece = occ.at[half_rows, pl.ds(pl.multiple_of(y * 128, 128), 128)]

    def occ1(k):
        return remote(occ_piece, oall.at[y, c, half_rows], o1s.at[k], o1r.at[k], r, col_to(k))

    def occ2(k):
        part = oall.at[y, :, half_rows]
        return remote(part, part, o2s.at[k], o2r.at[k], row_to(k), c)

    def occ3(k):
        part = oall.at[(y - k) & 3, :, half_rows]
        return remote(part, part, o3s.at[k], o3r.at[k], twin, c)

    def block(h, k):
        src = ints.at[pl.ds(h * 64 + col_to(k) * 4, 4)]
        return remote(src, mine.at[h, c], ms.at[h * 16 + k], mr.at[h * 16 + k], r, col_to(k))

    def quarter(u, k):
        dst = quart.at[r, pl.ds(u * 64, 64)]
        return remote(piece(y_to(k), u), dst, qs.at[u * 4 + k], qr.at[u * 4 + k], row_to(k), c)

    def forward(u, k):
        part = quart.at[((y - k) & 3) * 2 + core, pl.ds(u * 64, 64)]
        return remote(part, part, fs.at[u * 4 + k], fr.at[u * 4 + k], twin, c)

    def send_own(u):
        dst = quart.at[r, pl.ds(u * 64, 64)]
        return remote(piece(y, u), dst, fs.at[u * 4], fr.at[u * 4], twin, c)

    def send_w(h, k):
        yy, cc = y_to(k >> 4), col_to(k & 15)
        at = h * 64 + k
        return remote(wout.at[h, cc, yy], wgot.at[h, me], ws.at[at], wr.at[at], yy * 2 + core, cc)

    def send_part(k):
        yy, cc = y_to(k >> 4), col_to(k & 15)
        return remote(part.at[cc, yy], got.at[me], ps.at[0], pr.at[0], yy * 2 + core, cc)

    tables = [
        pltpu.make_async_copy(src, dst, loc.at[i])
        for i, (src, dst) in enumerate(((lists_in, lists), (owner_in, owner), (sizes_in, sizes)))
    ]
    own = [
        pltpu.make_async_copy(virt.at[half_rows], vall.at[c, half_rows], v1r.at[0]),
        pltpu.make_async_copy(occ_piece, oall.at[y, c, half_rows], o1r.at[0]),
        pltpu.make_async_copy(ints.at[pl.ds(c * 4, 4)], mine.at[0, c], mr.at[0]),
        pltpu.make_async_copy(ints.at[pl.ds(64 + c * 4, 4)], mine.at[1, c], mr.at[16]),
        pltpu.make_async_copy(piece(y, 0), quart.at[r, pl.ds(0, 64)], qr.at[0]),
        pltpu.make_async_copy(piece(y, 1), quart.at[r, pl.ds(64, 64)], qr.at[4]),
    ]
    for copy in tables + own:
        copy.start()

    barrier = pltpu.get_barrier_semaphore()

    def greet(row, col):
        pl.semaphore_signal(barrier, inc=1, device_id=(row, col), device_id_type=MESH)

    loop(1, 16, lambda k: greet(r, col_to(k)))
    loop(1, 4, lambda k: greet(row_to(k), c))
    greet(twin, c)

    pl.semaphore_wait(barrier, 19)
    for k in (2, 1, 3):
        quarter(0, k).start()
    for k in ORDER:
        virt1(k).start()
    for k in ORDER:
        occ1(k).start()
    for k in ORDER:
        block(0, k).start()
    send_own(0).start()

    for copy in tables:
        copy.wait()
    for s in range(16):
        atom = jnp.int32(0)
        for a in range(16):
            atom = jnp.where(owner[a] == s, a, atom)
        slot_size[s] = sizes[atom]
        for k in range(8):
            starts[s * 8 + k] = owner[lists[k, atom]]

    own[0].wait()
    loop(1, 16, lambda k: virt1(k).wait_recv())
    virt2().start()
    own[1].wait()
    loop(1, 16, lambda k: occ1(k).wait_recv())
    loop(1, 4, lambda k: occ2(k).start())
    occ3(0).start()
    for k in (2, 1, 3):
        quarter(1, k).start()
    send_own(1).start()

    def second(k):
        block(0, k).wait_send()
        block(1, k).start()

    for k in ORDER[:8]:
        second(k)
    virt2().wait_recv()

    lane = lax.broadcasted_iota(jnp.int32, (32, 512), 1)
    row = lax.broadcasted_iota(jnp.int32, (32, 512), 0)
    limit = jnp.zeros((32, 512), jnp.int32)
    for s in range(16):
        limit = jnp.where(lane // 32 == s, slot_size[s], limit)
    inside = lane % 32 < limit

    def mask(load, dst):
        def one(s):
            both = jnp.logical_and(inside, row < slot_size[s])
            dst[s] = jnp.where(both, load(s), jnp.zeros((), BF))

        loop(0, 16, one, 4)

    mask(lambda s: vall[s], veff)
    def pass_occ(k):
        occ2(k).wait_recv()
        occ3(k).start()

    loop(1, 4, pass_occ)
    for k in ORDER[8:]:
        second(k)

    def listed(ref, s):
        return jnp.concatenate([ref[starts[s * 8 + k]] for k in range(8)], axis=0)

    def make_left(h, i):
        dz = (2 + i) & 3
        zz = ((z - dz) & 3)
        for dx in range(4):
            arrived(mine.at[h, zz * 4 + ((x - dx) & 3)], mr.at[h * 16 + dz * 4 + dx])
        for xx in range(4):
            s = zz * 4 + xx
            res = jnp.dot(mine[h, s].reshape(128, 256), listed(veff, s), preferred_element_type=F32)
            left[:, xx * 32:(xx + 1) * 32, :] = res.astype(BF).reshape(4, 32, 512)
        for p in range(4):
            left_t[p, :, pl.ds(pl.multiple_of(zz * 128, 128), 128)] = left[p].T

    def make_w(h, k):
        t = col_to(k)
        lhs = left_t[:, pl.ds(pl.multiple_of(t * 32, 32), 32), :].reshape(128, 512)
        res = lax.dot_general(lhs, listed(oeff, t), NT, preferred_element_type=F32)
        res = res.astype(BF).reshape(4, 32, 256)
        for q in range(4):
            wout[h, t, q] = res[:, q // 2 * 16:q // 2 * 16 + 16, q % 2 * 128:q % 2 * 128 + 128]

    def pass_quarter(u):
        def one(k):
            quarter(u, k).wait_recv()
            forward(u, k).start()

        loop(1, 4, one)
        own[4 + u].wait()

    def lay_i(i):
        v = jnp.swapaxes(quart[i // 8, pl.ds(pl.multiple_of(i % 8 * 16, 16), 16)], 0, 1)
        for j in range(16):
            i2[pl.ds(pl.multiple_of(i * 16, 16), 16), j * 128:(j + 1) * 128] = v[j]

    def lay_piece(u, rr):
        loop(rr * 8 + u * 4, rr * 8 + u * 4 + 4, lay_i)

    def half(h):
        loop(0, 4, lambda i: make_left(h, i))

        @pl.when(h == 0)
        def _():
            loop(0, 4, lambda k: occ3(k).wait_recv())
            mask(lambda s: jnp.concatenate([oall[q, s] for q in range(4)], axis=1), oeff)

        for g in range(0, 16, 4):
            for k in MIXED[g:g + 4]:
                make_w(h, k)
            for k in MIXED[g:g + 4]:
                for dy in (2, 1, 3, 0):
                    if dy * 16 + k:
                        send_w(h, dy * 16 + k).start()
        pltpu.make_async_copy(wout.at[h, c, y], wgot.at[h, me], wr.at[h * 64]).start()

    loop(0, 2, half)

    pass_quarter(0)
    pass_quarter(1)

    def lay_other(u, k):
        forward(u, k).wait_recv()
        lay_piece(u, ((y - k) & 3) * 2 + 1 - core)

    loop(0, 4, lambda k: lay_piece(0, row_to(k)))
    loop(0, 4, lambda k: lay_piece(1, row_to(k)))
    loop(0, 4, lambda k: lay_other(0, k))
    loop(0, 4, lambda k: lay_other(1, k))

    def lay_w(h, i):
        dy, dz = i // 4, i % 4
        yy = ((y - dy) & 3)
        first = yy * 16 + ((z - dz) & 3) * 4
        for dx in range(4):
            arrived(wgot.at[h, first + ((x - dx) & 3)], wr.at[h * 64 + dy * 16 + dz * 4 + dx])
        v = jnp.swapaxes(wgot[h, pl.ds(first, 4)].reshape(16, 16, 128), 0, 1)
        at = (yy + h * (1 - 2 * (yy % 2))) * 64 + first % 16 * 4
        for j in range(16):
            w2[h, pl.ds(pl.multiple_of(at, 16), 16), j * 128:(j + 1) * 128] = v[j]

    def product(h, at, size):
        v = i2[pl.ds(pl.multiple_of(at, size), size), :]
        return lax.dot_general(v, w2[h], NT, preferred_element_type=F32).astype(BF)

    def multiply0(i):
        half0[pl.ds(pl.multiple_of(i * 512, 512), 512), :] = product(0, i * 512, 512)

    low = lax.broadcasted_iota(jnp.int32, (256, 128), 1) < 64

    def multiply1(dz):
        zz = (z + dz) & 3
        res = product(1, zz * 256, 256)
        old = half0[pl.ds(pl.multiple_of(zz * 256, 256), 256), :]
        for q in range(2):
            one, two = old[:, q * 128:(q + 1) * 128], res[:, q * 128:(q + 1) * 128]
            part[pl.ds(zz * 4, 4), q * 2] = jnp.where(low, one, two).reshape(4, 64, 128)
            part[pl.ds(zz * 4, 4), q * 2 + 1] = jnp.where(low, two, one).reshape(4, 64, 128)

    loop(0, 16, lambda i: lay_w(0, i))
    loop(0, 2, multiply0)
    loop(0, 16, lambda i: lay_w(1, i))
    for group in ((2,), (1, 3), (0,)):
        for dz in group:
            multiply1(dz)
        for dx in (2, 1, 3, 0):
            for dy in (2, 1, 3, 0):
                for dz in group:
                    k = dy * 16 + dz * 4 + dx
                    if k:
                        send_part(k).start()
    pltpu.make_async_copy(part.at[c, y], got.at[me], pr.at[0]).start()

    loop(1, 16, lambda k: (virt1(k).wait_send(), occ1(k).wait_send()))
    loop(1, 16, lambda k: block(1, k).wait_send())
    loop(1, 4, lambda k: (quarter(0, k).wait_send(), quarter(1, k).wait_send()))
    virt2().wait_send()
    loop(1, 4, lambda k: occ2(k).wait_send())
    loop(0, 4, lambda k: occ3(k).wait_send())
    loop(0, 4, lambda k: (forward(0, k).wait_send(), forward(1, k).wait_send()))
    loop(1, 64, lambda k: (send_w(0, k).wait_send(), send_w(1, k).wait_send()))
    arrived(got, pr.at[0])
    total = lax.fori_loop(0, 64, lambda i, acc: acc + got[i].astype(F32), jnp.zeros((64, 128), F32), unroll=4)
    out[...] = jnp.where((y & 1) == 1, pltpu.roll(total, 64, 1), total)

    arrived(got.at[pl.ds(0, 63)], ps.at[0])


def shards(integrals, virt_green, occ_green, block_list, block_owner, block_sizes):
    dma = pltpu.SemaphoreType.DMA
    vmem = pltpu.VMEM
    res = pl.pallas_call(
        kernel,
        out_shape=jax.ShapeDtypeStruct((64, 128), F32),
        in_specs=[ANY] * 6,
        out_specs=VMEM,
        scratch_shapes=[
            pltpu.SMEM((8, 16), jnp.int32),
            pltpu.SMEM((16,), jnp.int32),
            pltpu.SMEM((16,), jnp.int32),
            pltpu.SMEM((128,), jnp.int32),
            pltpu.SMEM((16,), jnp.int32),
            vmem((16, 32, 512), BF),
            vmem((4, 16, 32, 128), BF),
            vmem((2, 16, 4, 32, 256), BF),
            vmem((8, 128, 16, 128), BF),
            vmem((16, 32, 512), BF),
            vmem((16, 32, 512), BF),
            vmem((4, 128, 512), BF),
            vmem((4, 512, 512), BF),
            vmem((2, 16, 4, 4, 16, 128), BF),
            vmem((2, 64, 4, 16, 128), BF),
            vmem((1024, 2048), BF),
            vmem((2, 256, 2048), BF),
            vmem((1024, 256), BF),
            vmem((16, 4, 64, 128), BF),
            vmem((64, 64, 128), BF),
            dma((3,)), dma((16,)), dma((16,)), dma((1,)), dma((1,)),
            dma((16,)), dma((16,)), dma((4,)), dma((4,)), dma((4,)), dma((4,)),
            dma((32,)), dma((32,)), dma((8,)), dma((8,)), dma((8,)), dma((8,)),
            dma((128,)), dma((128,)), dma((1,)), dma((1,)),
        ],
        compiler_params=pltpu.CompilerParams(
            has_side_effects=True, collective_id=0, vmem_limit_bytes=63 << 20),
    )(block_list.T, block_owner, block_sizes, integrals, virt_green, occ_green)
    return res.T


def solution(mesh):
    in_specs = (P("row", "col", None), P("col", None), P("col", None), P(), P(), P())
    return jax.shard_map(shards, mesh=mesh, in_specs=in_specs, out_specs=P("row", "col"), check_vma=False)
```

```python
import jax
import jax.numpy as jnp
from jax import lax
from jax.experimental import pallas as pl
from jax.experimental.pallas import tpu as pltpu
from jax.sharding import PartitionSpec as P

BF = jnp.bfloat16
F32 = jnp.float32
ANY = pl.BlockSpec(memory_space=pl.ANY)
VMEM = pl.BlockSpec(memory_space=pltpu.VMEM)
SMEM = pl.BlockSpec(memory_space=pltpu.SMEM)
MESH = pl.DeviceIdType.MESH
NT = (((1,), (1,)), ((), ()))
ORDER = (10, 14, 6, 11, 9, 8, 2, 13, 7, 15, 5, 12, 4, 3, 1)
MIXED = (10, 1, 14, 4, 6, 3, 11, 12, 9, 2, 8, 5, 7, 13, 15, 0)


def loop(lo, hi, body, unroll=1):
    def step(i, carry):
        body(i)
        return carry

    lax.fori_loop(lo, hi, step, 0, unroll=unroll)


def remote(src, dst, ssem, rsem, row, col):
    return pltpu.make_async_remote_copy(
        src_ref=src, dst_ref=dst, send_sem=ssem, recv_sem=rsem, device_id=(row, col), device_id_type=MESH,
    )


def arrived(ref, sem):
    pltpu.make_async_copy(ref, ref, sem).wait()


def kernel(lists_in, owner_in, sizes_in, ints, virt, occ, out,
           lists, owner, sizes, starts, slot_size, vall, oall, mine, quart, veff, oeff, left, left_t, wout, wgot, i2, w2, half0, part, got,
           loc, v1s, v1r, v2s, v2r, o1s, o1r, o2s, o2r, o3s, o3r, ms, mr, qs, qr, fs, fr, ws, wr, ps, pr):
    r = lax.axis_index("row")
    c = lax.axis_index("col")
    y, core = r >> 1, r & 1
    z, x = c >> 2, c & 3
    me = y * 16 + c
    twin = y * 2 + (1 - core)

    cols = [((z + k // 4) & 3) * 4 + ((x + k % 4) & 3) for k in range(16)]
    ys = [(y + k) & 3 for k in range(4)]

    def col_to(k):
        return cols[k] if isinstance(k, int) else ((z + (k >> 2)) & 3) * 4 + ((x + (k & 3)) & 3)

    def y_to(k):
        return ys[k] if isinstance(k, int) else (y + k) & 3

    def row_to(k):
        return y_to(k) * 2 + core

    def piece(yy, u):
        return ints.at[pl.ds(u * 64, 64), pl.ds((yy >> 1) * 16, 16), pl.ds((yy & 1) * 128, 128)]

    half_rows = pl.ds(core * 16, 16)

    def virt1(k):
        return remote(virt.at[half_rows], vall.at[c, half_rows], v1s.at[k], v1r.at[k], r, col_to(k))

    def virt2():
        part = vall.at[:, half_rows]
        return remote(part, part, v2s.at[0], v2r.at[0], twin, c)

    occ_piece = occ.at[half_rows, pl.ds(pl.multiple_of(y * 128, 128), 128)]

    def occ1(k):
        return remote(occ_piece, oall.at[y, c, half_rows], o1s.at[k], o1r.at[k], r, col_to(k))

    def occ2(k):
        part = oall.at[y, :, half_rows]
        return remote(part, part, o2s.at[k], o2r.at[k], row_to(k), c)

    def occ3(k):
        part = oall.at[(y - k) & 3, :, half_rows]
        return remote(part, part, o3s.at[k], o3r.at[k], twin, c)

    def block(h, k):
        src = ints.at[pl.ds(h * 64 + col_to(k) * 4, 4)]
        return remote(src, mine.at[h, c], ms.at[h * 16 + k], mr.at[h * 16 + k], r, col_to(k))

    def quarter(u, k):
        dst = quart.at[r, pl.ds(u * 64, 64)]
        return remote(piece(y_to(k), u), dst, qs.at[u * 4 + k], qr.at[u * 4 + k], row_to(k), c)

    def forward(u, k):
        part = quart.at[((y - k) & 3) * 2 + core, pl.ds(u * 64, 64)]
        return remote(part, part, fs.at[u * 4 + k], fr.at[u * 4 + k], twin, c)

    def send_own(u):
        dst = quart.at[r, pl.ds(u * 64, 64)]
        return remote(piece(y, u), dst, fs.at[u * 4], fr.at[u * 4], twin, c)

    def send_w(h, k):
        yy, cc = y_to(k >> 4), col_to(k & 15)
        at = h * 64 + k
        return remote(wout.at[h, cc, yy], wgot.at[h, me], ws.at[at], wr.at[at], yy * 2 + core, cc)

    def send_part(k):
        yy, cc = y_to(k >> 4), col_to(k & 15)
        return remote(part.at[cc, yy], got.at[z * 16 + y * 4 + x], ps.at[0], pr.at[(k >> 2) & 3], yy * 2 + core, cc)

    tables = [
        pltpu.make_async_copy(src, dst, loc.at[i])
        for i, (src, dst) in enumerate(((lists_in, lists), (owner_in, owner), (sizes_in, sizes)))
    ]
    own = [
        pltpu.make_async_copy(virt.at[half_rows], vall.at[c, half_rows], v1r.at[0]),
        pltpu.make_async_copy(occ_piece, oall.at[y, c, half_rows], o1r.at[0]),
        pltpu.make_async_copy(ints.at[pl.ds(c * 4, 4)], mine.at[0, c], mr.at[0]),
        pltpu.make_async_copy(ints.at[pl.ds(64 + c * 4, 4)], mine.at[1, c], mr.at[16]),
        pltpu.make_async_copy(piece(y, 0), quart.at[r, pl.ds(0, 64)], qr.at[0]),
        pltpu.make_async_copy(piece(y, 1), quart.at[r, pl.ds(64, 64)], qr.at[4]),
    ]
    for copy in tables + own:
        copy.start()

    barrier = pltpu.get_barrier_semaphore()

    def greet(row, col):
        pl.semaphore_signal(barrier, inc=1, device_id=(row, col), device_id_type=MESH)

    loop(1, 16, lambda k: greet(r, col_to(k)))
    loop(1, 4, lambda k: greet(row_to(k), c))
    greet(twin, c)

    pl.semaphore_wait(barrier, 19)
    for k in (2, 1, 3):
        quarter(0, k).start()
    for k in ORDER:
        virt1(k).start()
    for k in ORDER:
        occ1(k).start()
    for k in ORDER:
        block(0, k).start()
    send_own(0).start()

    for copy in tables:
        copy.wait()
    for s in range(16):
        atom = jnp.int32(0)
        for a in range(16):
            atom = jnp.where(owner[a] == s, a, atom)
        slot_size[s] = sizes[atom]
        for k in range(8):
            starts[s * 8 + k] = owner[lists[k, atom]]

    own[0].wait()
    loop(1, 16, lambda k: virt1(k).wait_recv())
    virt2().start()
    own[1].wait()
    loop(1, 16, lambda k: occ1(k).wait_recv())
    loop(1, 4, lambda k: occ2(k).start())
    occ3(0).start()
    for k in (2, 1, 3):
        quarter(1, k).start()
    send_own(1).start()

    def second(k):
        block(0, k).wait_send()
        block(1, k).start()

    for k in ORDER[:8]:
        second(k)
    virt2().wait_recv()

    lane = lax.broadcasted_iota(jnp.int32, (32, 512), 1)
    row = lax.broadcasted_iota(jnp.int32, (32, 512), 0)
    limit = jnp.zeros((32, 512), jnp.int32)
    for s in range(16):
        limit = jnp.where(lane // 32 == s, slot_size[s], limit)
    inside = lane % 32 < limit

    def mask(load, dst):
        def one(s):
            both = jnp.logical_and(inside, row < slot_size[s])
            dst[s] = jnp.where(both, load(s), jnp.zeros((), BF))

        loop(0, 16, one, 4)

    mask(lambda s: vall[s], veff)
    def pass_occ(k):
        occ2(k).wait_recv()
        occ3(k).start()

    loop(1, 4, pass_occ)
    for k in ORDER[8:]:
        second(k)

    def listed(ref, s):
        return jnp.concatenate([ref[starts[s * 8 + k]] for k in range(8)], axis=0)

    def make_left(h, i):
        dz = (2 + i) & 3
        zz = ((z - dz) & 3)
        for dx in range(4):
            arrived(mine.at[h, zz * 4 + ((x - dx) & 3)], mr.at[h * 16 + dz * 4 + dx])
        for xx in range(4):
            s = zz * 4 + xx
            res = jnp.dot(mine[h, s].reshape(128, 256), listed(veff, s), preferred_element_type=F32)
            left[:, xx * 32:(xx + 1) * 32, :] = res.astype(BF).reshape(4, 32, 512)
        for p in range(4):
            left_t[p, :, pl.ds(pl.multiple_of(zz * 128, 128), 128)] = left[p].T

    def make_w(h, k):
        t = col_to(k)
        lhs = left_t[:, pl.ds(pl.multiple_of(t * 32, 32), 32), :].reshape(128, 512)
        res = lax.dot_general(lhs, listed(oeff, t), NT, preferred_element_type=F32)
        res = res.astype(BF).reshape(4, 32, 256)
        for q in range(4):
            wout[h, t, q] = res[:, q // 2 * 16:q // 2 * 16 + 16, q % 2 * 128:q % 2 * 128 + 128]

    def pass_quarter(u):
        def one(k):
            quarter(u, k).wait_recv()
            forward(u, k).start()

        loop(1, 4, one)
        own[4 + u].wait()

    def lay_i(i):
        v = jnp.swapaxes(quart[i // 8, pl.ds(pl.multiple_of(i % 8 * 16, 16), 16)], 0, 1)
        for j in range(16):
            i2[pl.ds(pl.multiple_of(i * 16, 16), 16), j * 128:(j + 1) * 128] = v[j]

    def lay_piece(u, rr):
        loop(rr * 8 + u * 4, rr * 8 + u * 4 + 4, lay_i)

    def half(h):
        loop(0, 4, lambda i: make_left(h, i))

        @pl.when(h == 0)
        def _():
            loop(0, 4, lambda k: occ3(k).wait_recv())
            mask(lambda s: jnp.concatenate([oall[q, s] for q in range(4)], axis=1), oeff)

        for g in range(0, 16, 4):
            for k in MIXED[g:g + 4]:
                make_w(h, k)
            for k in MIXED[g:g + 4]:
                for dy in (2, 1, 3, 0):
                    if dy * 16 + k:
                        send_w(h, dy * 16 + k).start()
        pltpu.make_async_copy(wout.at[h, c, y], wgot.at[h, me], wr.at[h * 64]).start()

    loop(0, 2, half)

    pass_quarter(0)
    pass_quarter(1)

    def lay_other(u, k):
        forward(u, k).wait_recv()
        lay_piece(u, ((y - k) & 3) * 2 + 1 - core)

    loop(0, 4, lambda k: lay_piece(0, row_to(k)))
    loop(0, 4, lambda k: lay_piece(1, row_to(k)))
    loop(0, 4, lambda k: lay_other(0, k))
    loop(0, 4, lambda k: lay_other(1, k))

    def lay_w(h, i):
        dy, dz = i // 4, i % 4
        yy = ((y - dy) & 3)
        first = yy * 16 + ((z - dz) & 3) * 4
        for dx in range(4):
            arrived(wgot.at[h, first + ((x - dx) & 3)], wr.at[h * 64 + dy * 16 + dz * 4 + dx])
        v = jnp.swapaxes(wgot[h, pl.ds(first, 4)].reshape(16, 16, 128), 0, 1)
        at = (yy + h * (1 - 2 * (yy % 2))) * 64 + first % 16 * 4
        for j in range(16):
            w2[h, pl.ds(pl.multiple_of(at, 16), 16), j * 128:(j + 1) * 128] = v[j]

    def product(h, at, size):
        v = i2[pl.ds(pl.multiple_of(at, size), size), :]
        return lax.dot_general(v, w2[h], NT, preferred_element_type=F32).astype(BF)

    def multiply0(i):
        half0[pl.ds(pl.multiple_of(i * 512, 512), 512), :] = product(0, i * 512, 512)

    low = lax.broadcasted_iota(jnp.int32, (256, 128), 1) < 64

    def multiply1(dz):
        zz = (z + dz) & 3
        res = product(1, zz * 256, 256)
        old = half0[pl.ds(pl.multiple_of(zz * 256, 256), 256), :]
        for q in range(2):
            one, two = old[:, q * 128:(q + 1) * 128], res[:, q * 128:(q + 1) * 128]
            part[pl.ds(zz * 4, 4), q * 2] = jnp.where(low, one, two).reshape(4, 64, 128)
            part[pl.ds(zz * 4, 4), q * 2 + 1] = jnp.where(low, two, one).reshape(4, 64, 128)

    loop(0, 16, lambda i: lay_w(0, i))
    loop(0, 2, multiply0)
    loop(0, 16, lambda i: lay_w(1, i))
    for group in ((2,), (1, 3), (0,)):
        for dz in group:
            multiply1(dz)
        for dx in (2, 1, 3, 0):
            for dy in (2, 1, 3, 0):
                for dz in group:
                    k = dy * 16 + dz * 4 + dx
                    if k:
                        send_part(k).start()
    pltpu.make_async_copy(part.at[c, y], got.at[z * 16 + y * 4 + x], pr.at[0]).start()

    loop(1, 16, lambda k: (virt1(k).wait_send(), occ1(k).wait_send()))
    loop(1, 16, lambda k: block(1, k).wait_send())
    loop(1, 4, lambda k: (quarter(0, k).wait_send(), quarter(1, k).wait_send()))
    virt2().wait_send()
    loop(1, 4, lambda k: occ2(k).wait_send())
    loop(0, 4, lambda k: occ3(k).wait_send())
    loop(0, 4, lambda k: (forward(0, k).wait_send(), forward(1, k).wait_send()))
    loop(1, 64, lambda k: (send_w(0, k).wait_send(), send_w(1, k).wait_send()))
    total = jnp.zeros((64, 128), F32)
    for dz in (2, 1, 3, 0):
        first = ((z - dz) & 3) * 16
        arrived(got.at[pl.ds(first, 16)], pr.at[dz])
        total = lax.fori_loop(0, 16, lambda i, acc, at=first: acc + got[at + i].astype(F32), total, unroll=16)
    out[...] = jnp.where((y & 1) == 1, pltpu.roll(total, 64, 1), total)

    arrived(got.at[pl.ds(0, 63)], ps.at[0])


def shards(integrals, virt_green, occ_green, block_list, block_owner, block_sizes):
    dma = pltpu.SemaphoreType.DMA
    vmem = pltpu.VMEM
    res = pl.pallas_call(
        kernel,
        out_shape=jax.ShapeDtypeStruct((64, 128), F32),
        in_specs=[ANY] * 6,
        out_specs=VMEM,
        scratch_shapes=[
            pltpu.SMEM((8, 16), jnp.int32),
            pltpu.SMEM((16,), jnp.int32),
            pltpu.SMEM((16,), jnp.int32),
            pltpu.SMEM((128,), jnp.int32),
            pltpu.SMEM((16,), jnp.int32),
            vmem((16, 32, 512), BF),
            vmem((4, 16, 32, 128), BF),
            vmem((2, 16, 4, 32, 256), BF),
            vmem((8, 128, 16, 128), BF),
            vmem((16, 32, 512), BF),
            vmem((16, 32, 512), BF),
            vmem((4, 128, 512), BF),
            vmem((4, 512, 512), BF),
            vmem((2, 16, 4, 4, 16, 128), BF),
            vmem((2, 64, 4, 16, 128), BF),
            vmem((1024, 2048), BF),
            vmem((2, 256, 2048), BF),
            vmem((1024, 256), BF),
            vmem((16, 4, 64, 128), BF),
            vmem((64, 64, 128), BF),
            dma((3,)), dma((16,)), dma((16,)), dma((1,)), dma((1,)),
            dma((16,)), dma((16,)), dma((4,)), dma((4,)), dma((4,)), dma((4,)),
            dma((32,)), dma((32,)), dma((8,)), dma((8,)), dma((8,)), dma((8,)),
            dma((128,)), dma((128,)), dma((1,)), dma((4,)),
        ],
        compiler_params=pltpu.CompilerParams(
            has_side_effects=True, collective_id=0, vmem_limit_bytes=63 << 20),
    )(block_list.T, block_owner, block_sizes, integrals, virt_green, occ_green)
    return res.T


def solution(mesh):
    in_specs = (P("row", "col", None), P("col", None), P("col", None), P(), P(), P())
    return jax.shard_map(shards, mesh=mesh, in_specs=in_specs, out_specs=P("row", "col"), check_vma=False)
```
